32 devices in a mesh: grid: 32 (over z, y, x, core), day: 1.
Axes of the slice: x: 2, y: 2, z: 4, core: 2. Of those that a mesh axis runs over, the one named last changes fastest.
Arguments:
- fields: bfloat16 [384, 131072], P('day', 'grid')
- eof_basis: bfloat16 [131072, 128], P('grid'), may hold values from -0.015625 to 0.015625
- seed_days: int32 [16], replicated, may hold values from 0 to 383, as said below
Outputs:
- memberships: float32 [384, 16], P('day')
- regime_centers: float32 [16, 128], replicated
- composites: float32 [16, 131072], P(None, 'grid')
The draws below stay inside these ranges and needn't reach their ends.
Inputs may be any that keep to these rules, and one draw needn't show every extreme that they name: `seed_days`: 16 distinct days of the record.
All inputs are finite; a program needn't handle non-finite values.
Results may differ from the reference program's by a relative error of at most 0.00043.
Values sent between devices are 32-bit elements; how exact they have to be, the bound alone decides.
A program may use at most 64 MiB of HBM per device.

```python
import jax
import jax.numpy as jnp
from jax import lax

K = 128
C = 16
ITERS = 3
DAYS = 384
G = 131072


def draw_fields(key, part):
    key_label = jax.random.fold_in(key, 11)
    key_pattern = jax.random.fold_in(key, 12)
    key_noise = jax.random.fold_in(key, 13)
    labels = jax.random.randint(key_label, (DAYS,), 0, C)
    patterns = jax.random.normal(key_pattern, (C, G), jnp.float32)
    noise = jax.random.normal(key_noise, (DAYS, G), jnp.float32)
    values = 1.5 * jnp.take(patterns, labels, axis=0) + noise
    return values.astype(jnp.bfloat16)


def draw_seed_days(key, part):
    inner = jax.random.permutation(jax.random.fold_in(key, 21), DAYS - 2)[:C - 2].astype(jnp.int32) + 1
    ends = jnp.array([0, DAYS - 1], dtype=jnp.int32)
    chosen = jnp.concatenate([ends, inner])
    order = jax.random.permutation(jax.random.fold_in(key, 22), C)
    return chosen[order].astype(jnp.int32)


def block_scale(own_key, dims, cuts, smallest, top_value):
    loudness = 1.0
    for dim, parts in cuts:
        heights = jax.random.uniform(jax.random.fold_in(jax.random.fold_in(own_key, 6), dim), (parts,), jnp.float32, smallest / len(cuts), top_value / len(cuts))
        loudness = loudness * jnp.repeat(jnp.exp(heights), dims[dim] // parts).reshape((-1,) + (1,) * (len(dims) - 1 - dim))
    return loudness


def bell_draw(own_key, extent, width, reach, shards=(), kind=jnp.bfloat16):
    values = width * jax.random.normal(own_key, extent, jnp.float32)
    if shards:
        values = values * block_scale(own_key, extent, shards, -0.22, 0.18)
    return jnp.clip(values, -reach, reach).astype(kind)


def setup_inputs(seed: int = 0) -> dict:
    arg_keys = jax.random.split(jax.random.key(seed), 4)
    fields = draw_fields(jax.random.fold_in(arg_keys[3], 71), 0)
    eof_basis = bell_draw(arg_keys[1], (G, K), G ** -0.5, 0.015625, ((0, 32),))
    seed_days = draw_seed_days(jax.random.fold_in(arg_keys[3], 71), 0)
    return dict(fields=fields, eof_basis=eof_basis, seed_days=seed_days)


def member_of(amplitudes, centers):
    offsets = amplitudes[:, None, :] - centers[None, :, :]
    mean_square = jnp.mean(offsets * offsets, axis=2) + 1e-5
    weights = 1.0 / mean_square
    return weights / jnp.sum(weights, axis=1, keepdims=True)


def reference(fields, eof_basis, seed_days):
    amplitudes = jnp.dot(fields, eof_basis, preferred_element_type=jnp.float32)
    centers = jnp.take(amplitudes, seed_days.astype(jnp.int32), axis=0)
    for sweep in range(ITERS):
        member = member_of(amplitudes, centers)
        squared = member * member
        numerator = jnp.dot(squared.T, amplitudes, precision=lax.Precision.HIGHEST)
        centers = numerator / jnp.sum(squared, axis=0)[:, None]
    memberships = member_of(amplitudes, centers)
    squares = memberships * memberships
    weights_bf = squares.astype(jnp.bfloat16)
    numerator = jnp.dot(weights_bf.T, fields, preferred_element_type=jnp.float32)
    composites = numerator / jnp.sum(squares, axis=0)[:, None]
    return memberships, centers, composites
```

```python
import functools

import jax
import jax.numpy as jnp
from jax import lax
from jax.experimental import pallas as pl
from jax.experimental.pallas import tpu as pltpu
from jax.sharding import PartitionSpec as P

ITERS = 3
CHUNKS = 2
VMEM_BYTES = 48 * 1024 * 1024
NT = (((1,), (1,)), ((), ()))


def member_of(amplitudes, centers):
    offsets = amplitudes[:, None, :] - centers[None, :, :]
    mean_square = jnp.mean(offsets * offsets, axis=2) + 1e-05
    weights = 1.0 / mean_square
    return weights / jnp.sum(weights, axis=1, keepdims=True)


def seed_terms(seed_days, first, amplitudes):
    positions = first + jnp.arange(amplitudes.shape[0], dtype=jnp.int32)
    selector = (seed_days[:, None] == positions[None, :]).astype(jnp.float32)
    return jnp.dot(selector, amplitudes, precision=lax.Precision.HIGHEST)


def regime_terms(amplitudes, centers):
    member = member_of(amplitudes, centers)
    squared = member * member
    numerator = jnp.dot(squared.T, amplitudes, precision=lax.Precision.HIGHEST)
    return (numerator, jnp.sum(squared, axis=0))


def amplitude_kernel(n, fields, basis, out, fbuf, bbuf, give, take, mine, parts, gathered,
                     load_sems, pair_sems, scatter_send, scatter_recv, gather_send, gather_recv):
    pairs = n // 2
    rows = out.shape[0]
    half = rows // 2
    piece = half // CHUNKS
    block = rows // n
    me = lax.axis_index("grid")
    core = lax.rem(me, 2)
    spot = me // 2
    partner = me + 1 - 2 * core

    def at(other_spot):
        return {"grid": 2 * other_spot + core}

    barrier = pltpu.get_barrier_semaphore()
    pl.semaphore_signal(barrier, inc=1, device_id={"grid": partner}, device_id_type=pl.DeviceIdType.MESH)
    for step in range(1, pairs):
        pl.semaphore_signal(barrier, inc=1, device_id=at(lax.rem(spot + step, pairs)),
                            device_id_type=pl.DeviceIdType.MESH)

    basis_load = pltpu.make_async_copy(basis, bbuf, load_sems.at[2 * CHUNKS])
    basis_load.start()
    loads = []
    for i in range(2 * CHUNKS):
        side = 1 - core if i < CHUNKS else core
        first = pl.multiple_of(side * half + (i % CHUNKS) * piece, 16)
        load = pltpu.make_async_copy(fields.at[pl.ds(first, piece)], fbuf.at[pl.ds(i * piece, piece)],
                                     load_sems.at[i])
        load.start()
        loads.append(load)
    basis_load.wait()

    def product(i):
        loads[i].wait()
        return jnp.dot(fbuf[i * piece:(i + 1) * piece, :], bbuf[...], preferred_element_type=jnp.float32)

    for i in range(CHUNKS):
        give[i * piece:(i + 1) * piece, :] = product(i)
    pl.semaphore_wait(barrier, pairs)
    pair_give = pltpu.make_async_remote_copy(
        src_ref=give, dst_ref=take, send_sem=pair_sems.at[0], recv_sem=pair_sems.at[1],
        device_id={"grid": partner}, device_id_type=pl.DeviceIdType.MESH)
    pair_give.start()
    own = [product(CHUNKS + i) for i in range(CHUNKS)]
    pair_give.wait_recv()
    total = jnp.concatenate(own, axis=0) + take[...]
    for j in range(pairs):
        mine[j] = total[j * block:(j + 1) * block, :]

    scatters = []
    for step in range(1, pairs):
        to = lax.rem(spot + step, pairs)
        copy = pltpu.make_async_remote_copy(
            src_ref=mine.at[to], dst_ref=parts.at[spot], send_sem=scatter_send.at[step],
            recv_sem=scatter_recv.at[spot], device_id=at(to), device_id_type=pl.DeviceIdType.MESH)
        copy.start()
        scatters.append(copy)
    parts[spot] = mine[spot]
    for step in range(1, pairs):
        source = lax.rem(spot + pairs - step, pairs)
        pltpu.make_async_remote_copy(
            src_ref=mine.at[source], dst_ref=parts.at[source], send_sem=scatter_send.at[step],
            recv_sem=scatter_recv.at[source], device_id=at(source),
            device_id_type=pl.DeviceIdType.MESH).wait_recv()
    gathered[core, spot] = jnp.sum(parts[...], axis=0)

    gathers = []
    for step in range(1, pairs):
        to = lax.rem(spot + step, pairs)
        copy = pltpu.make_async_remote_copy(
            src_ref=gathered.at[core, spot], dst_ref=gathered.at[core, spot], send_sem=gather_send.at[step],
            recv_sem=gather_recv.at[spot], device_id=at(to), device_id_type=pl.DeviceIdType.MESH)
        copy.start()
        gathers.append(copy)
    for step in range(1, pairs):
        source = lax.rem(spot + pairs - step, pairs)
        pltpu.make_async_remote_copy(
            src_ref=gathered.at[core, source], dst_ref=gathered.at[core, source],
            send_sem=gather_send.at[step], recv_sem=gather_recv.at[source], device_id=at(source),
            device_id_type=pl.DeviceIdType.MESH).wait_recv()
    pair_back = pltpu.make_async_remote_copy(
        src_ref=gathered.at[core], dst_ref=gathered.at[core], send_sem=pair_sems.at[2],
        recv_sem=pair_sems.at[3], device_id={"grid": partner}, device_id_type=pl.DeviceIdType.MESH)
    pair_back.start()
    pltpu.make_async_remote_copy(
        src_ref=gathered.at[1 - core], dst_ref=gathered.at[1 - core], send_sem=pair_sems.at[2],
        recv_sem=pair_sems.at[3], device_id={"grid": partner},
        device_id_type=pl.DeviceIdType.MESH).wait_recv()
    for side in range(2):
        for j in range(pairs):
            first = side * half + j * block
            out[first:first + block, :] = gathered[side, j]
    pair_give.wait_send()
    pair_back.wait_send()
    for copy in scatters + gathers:
        copy.wait_send()


def summed_amplitudes(n, fields, basis):
    rows, depth = fields.shape
    eofs = basis.shape[1]
    pairs, half, block = n // 2, rows // 2, rows // n
    return pl.pallas_call(
        functools.partial(amplitude_kernel, n),
        out_shape=jax.ShapeDtypeStruct((rows, eofs), jnp.float32),
        in_specs=[pl.BlockSpec(memory_space=pl.ANY)] * 2,
        out_specs=pl.BlockSpec(memory_space=pltpu.VMEM),
        scratch_shapes=[
            pltpu.VMEM((rows, depth), jnp.bfloat16),
            pltpu.VMEM((depth, eofs), jnp.bfloat16),
            pltpu.VMEM((half, eofs), jnp.float32),
            pltpu.VMEM((half, eofs), jnp.float32),
            pltpu.VMEM((pairs, block, eofs), jnp.float32),
            pltpu.VMEM((pairs, block, eofs), jnp.float32),
            pltpu.VMEM((2, pairs, block, eofs), jnp.float32),
            pltpu.SemaphoreType.DMA((2 * CHUNKS + 1,)),
            pltpu.SemaphoreType.DMA((4,)),
            pltpu.SemaphoreType.DMA((pairs,)),
            pltpu.SemaphoreType.DMA((pairs,)),
            pltpu.SemaphoreType.DMA((pairs,)),
            pltpu.SemaphoreType.DMA((pairs,)),
        ],
        compiler_params=pltpu.CompilerParams(
            collective_id=0, has_side_effects=True, vmem_limit_bytes=VMEM_BYTES),
        cost_estimate=pl.CostEstimate(
            flops=2 * rows * depth * eofs, bytes_accessed=2 * depth * (rows + eofs), transcendentals=0),
    )(fields, basis)


def split(value, pieces):
    out = []
    for _ in range(pieces):
        part = value.astype(jnp.bfloat16)
        out.append(part)
        value = value - part.astype(jnp.float32)
    return out


def regime_kernel(seeds, amplitudes, fields, member_out, centers_out, composites, fbuf, load_sems):
    days, eofs = amplitudes.shape
    regimes = centers_out.shape[0]
    piece = days // CHUNKS
    loads = []
    for i in range(CHUNKS):
        load = pltpu.make_async_copy(fields.at[pl.ds(i * piece, piece)], fbuf.at[pl.ds(i * piece, piece)],
                                     load_sems.at[i])
        load.start()
        loads.append(load)

    turned = amplitudes[...].T
    with_ones = jnp.concatenate([turned, jnp.ones((8, days), jnp.float32)], axis=0)
    first, second, third = split(with_ones, 3)
    exact = jnp.concatenate([first, second, third], axis=1)
    five = jnp.concatenate([exact, first, second], axis=1)

    def member(columns):
        squares = []
        for c in range(regimes):
            offset = turned - columns[:, c:c + 1]
            squares.append(jnp.sum(offset * offset, axis=0, keepdims=True))
        mean_square = jnp.concatenate(squares, axis=0) * (1.0 / eofs) + 1e-05
        weights = 1.0 / mean_square
        return weights / jnp.sum(weights, axis=0, keepdims=True)

    positions = lax.broadcasted_iota(jnp.int32, (regimes, days), 1)
    selector = (seeds[...] == positions).astype(jnp.bfloat16)
    columns = lax.dot_general(exact, jnp.concatenate([selector] * 3, axis=1), NT,
                              preferred_element_type=jnp.float32)[:eofs]
    for sweep in range(ITERS):
        q = member(columns)
        high, low = split(q * q, 2)
        weights = jnp.concatenate([high, high, high, low, low], axis=1)
        sums = lax.dot_general(five, weights, NT, preferred_element_type=jnp.float32)
        columns = sums[:eofs] / sums[eofs:eofs + 1]
        if sweep == ITERS - 1:
            flat = lax.dot_general(weights, five, NT, preferred_element_type=jnp.float32)
            centers_out[...] = flat[:, :eofs] / flat[:, eofs:eofs + 1]
    final = member(columns)
    squares = final * final
    scale = 1.0 / jnp.sum(squares, axis=1, keepdims=True)
    weights_bf = squares.astype(jnp.bfloat16)
    member_out[...] = final.T
    for load in loads:
        load.wait()
    composites[...] = jnp.dot(weights_bf, fbuf[...], preferred_element_type=jnp.float32) * scale


def regimes_of(seed_days, amplitudes, fields):
    days, points = fields.shape
    eofs = amplitudes.shape[1]
    regimes = seed_days.shape[0]
    vmem = pl.BlockSpec(memory_space=pltpu.VMEM)
    return pl.pallas_call(
        regime_kernel,
        out_shape=(
            jax.ShapeDtypeStruct((days, regimes), jnp.float32),
            jax.ShapeDtypeStruct((regimes, eofs), jnp.float32),
            jax.ShapeDtypeStruct((regimes, points), jnp.float32),
        ),
        in_specs=[vmem, vmem, pl.BlockSpec(memory_space=pl.ANY)],
        out_specs=(vmem, vmem, vmem),
        scratch_shapes=[
            pltpu.VMEM((days, points), jnp.bfloat16),
            pltpu.SemaphoreType.DMA((CHUNKS,)),
        ],
        compiler_params=pltpu.CompilerParams(vmem_limit_bytes=VMEM_BYTES),
        cost_estimate=pl.CostEstimate(
            flops=2 * regimes * days * points, bytes_accessed=2 * days * points, transcendentals=0),
    )(seed_days.reshape(regimes, 1), amplitudes, fields)


def on_device(mesh, fields, eof_basis, seed_days):
    n = mesh.shape["grid"]
    day_rows = fields.shape[0]
    if n % 2 == 0 and n >= 4 and day_rows % (32 * CHUNKS) == 0 and day_rows % n == 0:
        amplitudes = summed_amplitudes(n, fields, eof_basis)
    else:
        partial_value = jnp.dot(fields, eof_basis, preferred_element_type=jnp.float32)
        amplitudes = lax.psum(partial_value, "grid")
    if mesh.shape["day"] == 1 and day_rows % 128 == 0 and eof_basis.shape[1] % 128 == 0:
        return regimes_of(seed_days, amplitudes, fields)
    first = lax.axis_index("day") * day_rows
    centers = lax.psum(seed_terms(seed_days, first, amplitudes), "day")
    for sweep in range(ITERS):
        numerator, denominator = lax.psum(regime_terms(amplitudes, centers), "day")
        centers = numerator / denominator[:, None]
    member_all = member_of(amplitudes, centers)
    squares = member_all * member_all
    weights_bf = squares.astype(jnp.bfloat16)
    weighted = jnp.dot(weights_bf.T, fields, preferred_element_type=jnp.float32)
    totals, weight_sums = lax.psum((weighted, jnp.sum(squares, axis=0)), "day")
    return (member_all, centers, totals / weight_sums[:, None])


def solution(mesh):
    placed = (P("day", "grid"), P("grid", None), P())
    return jax.shard_map(
        functools.partial(on_device, mesh),
        mesh=mesh,
        in_specs=placed,
        out_specs=(P("day", None), P(), P(None, "grid")),
        check_vma=False,
    )
```

```python
import functools

import jax
import jax.numpy as jnp
from jax import lax
from jax.experimental import pallas as pl
from jax.experimental.pallas import tpu as pltpu
from jax.sharding import PartitionSpec as P

ITERS = 3
CHUNKS = 2
VMEM_BYTES = 63 * 1024 * 1024 + 512 * 1024
NT = (((1,), (1,)), ((), ()))


def member_of(amplitudes, centers):
    offsets = amplitudes[:, None, :] - centers[None, :, :]
    mean_square = jnp.mean(offsets * offsets, axis=2) + 1e-05
    weights = 1.0 / mean_square
    return weights / jnp.sum(weights, axis=1, keepdims=True)


def seed_terms(seed_days, first, amplitudes):
    positions = first + jnp.arange(amplitudes.shape[0], dtype=jnp.int32)
    selector = (seed_days[:, None] == positions[None, :]).astype(jnp.float32)
    return jnp.dot(selector, amplitudes, precision=lax.Precision.HIGHEST)


def regime_terms(amplitudes, centers):
    member = member_of(amplitudes, centers)
    squared = member * member
    numerator = jnp.dot(squared.T, amplitudes, precision=lax.Precision.HIGHEST)
    return (numerator, jnp.sum(squared, axis=0))


def amplitude_kernel(lines, fields, basis, out, fbuf, bbuf, give, take, mine, parts, stack, load_sems,
                     pair_send, pair_recv, plane_send, plane_recv, line_send, line_recv,
                     back_send, back_recv, final_send, final_recv):
    rows = out.shape[0]
    half = rows // 2
    block = half // 4
    piece = 2 * block
    me = lax.axis_index("grid")
    core = lax.rem(me, 2)
    spot = me // 2
    plane = lax.rem(spot, 4)
    line = spot // 4
    px, py = lax.rem(plane, 2), plane // 2
    order = [(1 - py) * 2 + 1 - px, (1 - py) * 2 + px, py * 2 + 1 - px, plane]

    def send(src, dst, send_sem, recv_sem, device):
        return pltpu.make_async_remote_copy(
            src_ref=src, dst_ref=dst, send_sem=send_sem, recv_sem=recv_sem,
            device_id={"grid": device}, device_id_type=pl.DeviceIdType.MESH)

    partner = me + 1 - 2 * core
    plane_peers = [(line * 4 + position) * 2 + core for position in order[:3]]
    line_steps = sorted(range(1, lines), key=lambda step: -min(step, lines - step))
    line_peers = [lax.rem(line + step, lines) for step in line_steps]
    line_devices = [(peer * 4 + plane) * 2 + core for peer in line_peers]

    barrier = pltpu.get_barrier_semaphore()
    for device in [partner] + plane_peers + line_devices:
        pl.semaphore_signal(barrier, inc=1, device_id={"grid": device}, device_id_type=pl.DeviceIdType.MESH)

    basis_load = pltpu.make_async_copy(basis, bbuf, load_sems.at[8])
    basis_load.start()
    loads = []
    for i in range(8):
        side = 1 - core if i < 4 else core
        first = pl.multiple_of(side * half + order[i % 4] * block, 16)
        load = pltpu.make_async_copy(fields.at[pl.ds(first, block)], fbuf.at[pl.ds(i * block, block)],
                                     load_sems.at[i])
        load.start()
        loads.append(load)
    basis_load.wait()

    def product(i):
        loads[2 * i].wait()
        loads[2 * i + 1].wait()
        return jnp.dot(fbuf[i * piece:(i + 1) * piece, :], bbuf[...], preferred_element_type=jnp.float32)

    started = []
    pair_copies = []
    for i in range(2):
        part = pl.ds(i * piece, piece)
        give[part, :] = product(i)
        if i == 0:
            pl.semaphore_wait(barrier, 1 + 3 + lines - 1)
        copy = send(give.at[part], take.at[part], pair_send.at[i], pair_recv.at[i], partner)
        copy.start()
        pair_copies.append(copy)
    plane_copies = []
    for i in range(2):
        part = pl.ds(i * piece, piece)
        own = product(2 + i)
        pair_copies[i].wait_recv()
        mine[part, :] = own + take[part, :]
        for k in (2 * i, 2 * i + 1):
            if k < 3:
                copy = send(mine.at[pl.ds(k * block, block)], parts.at[k], plane_send.at[k], plane_recv.at[k],
                            plane_peers[k])
                copy.start()
                plane_copies.append(copy)
    total = mine[3 * block:, :]
    for k in (2, 1, 0):
        plane_copies[k].wait_recv()
        total = total + parts[k]
    stack[line] = total

    for step, device in enumerate(line_devices):
        copy = send(stack.at[line], stack.at[line], line_send.at[step], line_recv.at[line], device)
        copy.start()
        started.append(copy)
    for step in range(lines - 1):
        source = lax.rem(line + lines - line_steps[step], lines)
        send(stack.at[source], stack.at[source], line_send.at[step], line_recv.at[source],
             (source * 4 + plane) * 2 + core).wait_recv()
    total = stack[0]
    for j in range(1, lines):
        total = total + stack[j]

    def place(side, position):
        return out.at[pl.ds(pl.multiple_of(side * half + position * block, 8), block)]

    place(core, plane)[...] = total
    back_copies = []
    for k in range(3):
        copy = send(place(core, plane), place(core, plane), back_send.at[k], back_recv.at[k], plane_peers[k])
        copy.start()
        back_copies.append(copy)
    for k in (3, 2, 1, 0):
        if k < 3:
            send(place(core, order[k]), place(core, order[k]), back_send.at[k], back_recv.at[k],
                 plane_peers[k]).wait_recv()
        copy = send(place(core, order[k]), place(core, order[k]), final_send.at[k], final_recv.at[k], partner)
        copy.start()
        started.append(copy)
    for k in (3, 2, 1, 0):
        send(place(1 - core, order[k]), place(1 - core, order[k]), final_send.at[k], final_recv.at[k],
             partner).wait_recv()
    for copy in pair_copies + plane_copies + started + back_copies:
        copy.wait_send()


def summed_amplitudes(lines, fields, basis):
    rows, depth = fields.shape
    eofs = basis.shape[1]
    half, block = rows // 2, rows // 8
    dma = pltpu.SemaphoreType.DMA
    return pl.pallas_call(
        functools.partial(amplitude_kernel, lines),
        out_shape=jax.ShapeDtypeStruct((rows, eofs), jnp.float32),
        in_specs=[pl.BlockSpec(memory_space=pltpu.HBM)] * 2,
        out_specs=pl.BlockSpec(memory_space=pltpu.VMEM),
        scratch_shapes=[
            pltpu.VMEM((rows, depth), jnp.bfloat16),
            pltpu.VMEM((depth, eofs), jnp.bfloat16),
            pltpu.VMEM((half, eofs), jnp.float32),
            pltpu.VMEM((half, eofs), jnp.float32),
            pltpu.VMEM((half, eofs), jnp.float32),
            pltpu.VMEM((3, block, eofs), jnp.float32),
            pltpu.VMEM((lines, block, eofs), jnp.float32),
            dma((9,)), dma((2,)), dma((2,)), dma((3,)), dma((3,)), dma((lines,)), dma((lines,)),
            dma((3,)), dma((3,)), dma((4,)), dma((4,)),
        ],
        compiler_params=pltpu.CompilerParams(
            collective_id=0, has_side_effects=True, vmem_limit_bytes=VMEM_BYTES),
        cost_estimate=pl.CostEstimate(
            flops=2 * rows * depth * eofs, bytes_accessed=2 * depth * (rows + eofs), transcendentals=0),
    )(fields, basis)


def split(value, pieces):
    out = []
    for _ in range(pieces):
        part = value.astype(jnp.bfloat16)
        out.append(part)
        value = value - part.astype(jnp.float32)
    return out


def regime_kernel(seeds, amplitudes, fields, member_out, centers_out, composites, fbuf, load_sems):
    days, eofs = amplitudes.shape
    regimes = centers_out.shape[0]
    piece = days // CHUNKS
    loads = []
    for i in range(CHUNKS):
        load = pltpu.make_async_copy(fields.at[pl.ds(i * piece, piece)], fbuf.at[pl.ds(i * piece, piece)],
                                     load_sems.at[i])
        load.start()
        loads.append(load)

    turned = amplitudes[...].T
    with_ones = jnp.concatenate([turned, jnp.ones((8, days), jnp.float32)], axis=0)
    first, second, third = split(with_ones, 3)
    exact = jnp.concatenate([first, second, third], axis=1)
    five = jnp.concatenate([exact, first, second], axis=1)

    def member(columns):
        squares = []
        for c in range(regimes):
            offset = turned - columns[:, c:c + 1]
            squares.append(jnp.sum(offset * offset, axis=0, keepdims=True))
        mean_square = jnp.concatenate(squares, axis=0) * (1.0 / eofs) + 1e-05
        weights = 1.0 / mean_square
        return weights / jnp.sum(weights, axis=0, keepdims=True)

    positions = lax.broadcasted_iota(jnp.int32, (regimes, days), 1)
    rows = lax.broadcasted_iota(jnp.int32, (regimes, days), 0)
    chosen = jnp.zeros((regimes, days), jnp.int32)
    for c in range(regimes):
        chosen = jnp.where(rows == c, seeds[c], chosen)
    selector = (chosen == positions).astype(jnp.bfloat16)
    columns = lax.dot_general(exact, jnp.concatenate([selector] * 3, axis=1), NT,
                              preferred_element_type=jnp.float32)[:eofs]
    for sweep in range(ITERS):
        q = member(columns)
        high, low = split(q * q, 2)
        weights = jnp.concatenate([high, high, high, low, low], axis=1)
        sums = lax.dot_general(five, weights, NT, preferred_element_type=jnp.float32)
        columns = sums[:eofs] / sums[eofs:eofs + 1]
        if sweep == ITERS - 1:
            flat = lax.dot_general(weights, five, NT, preferred_element_type=jnp.float32)
            centers_out[...] = flat[:, :eofs] / flat[:, eofs:eofs + 1]
    final = member(columns)
    squares = final * final
    scale = 1.0 / jnp.sum(squares, axis=1, keepdims=True)
    weights_bf = squares.astype(jnp.bfloat16)
    member_out[...] = final
    for load in loads:
        load.wait()
    composites[...] = jnp.dot(weights_bf, fbuf[...], preferred_element_type=jnp.float32) * scale


def regimes_of(seed_days, amplitudes, fields):
    days, points = fields.shape
    eofs = amplitudes.shape[1]
    regimes = seed_days.shape[0]
    vmem = pl.BlockSpec(memory_space=pltpu.VMEM)
    member, centers, composites = pl.pallas_call(
        regime_kernel,
        out_shape=(
            jax.ShapeDtypeStruct((regimes, days), jnp.float32),
            jax.ShapeDtypeStruct((regimes, eofs), jnp.float32),
            jax.ShapeDtypeStruct((regimes, points), jnp.float32),
        ),
        in_specs=[pl.BlockSpec(memory_space=pltpu.SMEM), vmem, pl.BlockSpec(memory_space=pltpu.HBM)],
        out_specs=(vmem, vmem, vmem),
        scratch_shapes=[
            pltpu.VMEM((days, points), jnp.bfloat16),
            pltpu.SemaphoreType.DMA((CHUNKS,)),
        ],
        compiler_params=pltpu.CompilerParams(vmem_limit_bytes=VMEM_BYTES),
        cost_estimate=pl.CostEstimate(
            flops=2 * regimes * days * points, bytes_accessed=2 * days * points, transcendentals=0),
    )(seed_days, amplitudes, fields)
    return member.T, centers, composites


def on_device(mesh, fields, eof_basis, seed_days):
    n = mesh.shape["grid"]
    day_rows = fields.shape[0]
    if n % 8 == 0 and n > 8 and day_rows % 128 == 0:
        amplitudes = summed_amplitudes(n // 8, fields, eof_basis)
    else:
        partial_value = jnp.dot(fields, eof_basis, preferred_element_type=jnp.float32)
        amplitudes = lax.psum(partial_value, "grid")
    if mesh.shape["day"] == 1 and day_rows % 128 == 0 and eof_basis.shape[1] % 128 == 0:
        return regimes_of(seed_days, amplitudes, fields)
    first = lax.axis_index("day") * day_rows
    centers = lax.psum(seed_terms(seed_days, first, amplitudes), "day")
    for sweep in range(ITERS):
        numerator, denominator = lax.psum(regime_terms(amplitudes, centers), "day")
        centers = numerator / denominator[:, None]
    member_all = member_of(amplitudes, centers)
    squares = member_all * member_all
    weights_bf = squares.astype(jnp.bfloat16)
    weighted = jnp.dot(weights_bf.T, fields, preferred_element_type=jnp.float32)
    totals, weight_sums = lax.psum((weighted, jnp.sum(squares, axis=0)), "day")
    return (member_all, centers, totals / weight_sums[:, None])


def solution(mesh):
    placed = (P("day", "grid"), P("grid", None), P())
    return jax.shard_map(
        functools.partial(on_device, mesh),
        mesh=mesh,
        in_specs=placed,
        out_specs=(P("day", None), P(), P(None, "grid")),
        check_vma=False,
    )
```

```python
import functools

import jax
import jax.numpy as jnp
from jax import lax
from jax.experimental import pallas as pl
from jax.experimental.pallas import tpu as pltpu
from jax.sharding import PartitionSpec as P

ITERS = 3
CHUNKS = 2
VMEM_BYTES = 53 * 1024 * 1024
COLUMNS = 1024
NT = (((1,), (1,)), ((), ()))


def member_of(amplitudes, centers):
    offsets = amplitudes[:, None, :] - centers[None, :, :]
    mean_square = jnp.mean(offsets * offsets, axis=2) + 1e-05
    weights = 1.0 / mean_square
    return weights / jnp.sum(weights, axis=1, keepdims=True)


def seed_terms(seed_days, first, amplitudes):
    positions = first + jnp.arange(amplitudes.shape[0], dtype=jnp.int32)
    selector = (seed_days[:, None] == positions[None, :]).astype(jnp.float32)
    return jnp.dot(selector, amplitudes, precision=lax.Precision.HIGHEST)


def regime_terms(amplitudes, centers):
    member = member_of(amplitudes, centers)
    squared = member * member
    numerator = jnp.dot(squared.T, amplitudes, precision=lax.Precision.HIGHEST)
    return (numerator, jnp.sum(squared, axis=0))


def piece_sizes(block):
    return [block - 16, 16] if block > 16 else [block]


def amplitude_kernel(lines, fields, basis, out, fbuf, bbuf, give, take, mine, parts, stack, load_sems,
                     pair_send, pair_recv, plane_send, plane_recv, line_send, line_recv,
                     back_send, back_recv, final_send, final_recv):
    rows = out.shape[0]
    half = rows // 2
    block = half // 4
    me = lax.axis_index("grid")
    core = lax.rem(me, 2)
    spot = me // 2
    plane = lax.rem(spot, 4)
    line = spot // 4
    px, py = lax.rem(plane, 2), plane // 2
    order = [(1 - py) * 2 + 1 - px, (1 - py) * 2 + px, py * 2 + 1 - px, plane]

    def send(src, dst, send_sem, recv_sem, device):
        return pltpu.make_async_remote_copy(
            src_ref=src, dst_ref=dst, send_sem=send_sem, recv_sem=recv_sem,
            device_id={"grid": device}, device_id_type=pl.DeviceIdType.MESH)

    partner = me + 1 - 2 * core
    plane_peers = [(line * 4 + position) * 2 + core for position in order[:3]]
    line_steps = sorted(range(1, lines), key=lambda step: -min(step, lines - step))
    line_devices = [(lax.rem(line + step, lines) * 4 + plane) * 2 + core for step in line_steps]
    line_sources = [lax.rem(line + lines - step, lines) for step in line_steps]

    barrier = pltpu.get_barrier_semaphore()
    for device in [partner] + plane_peers + line_devices:
        pl.semaphore_signal(barrier, inc=1, device_id={"grid": device}, device_id_type=pl.DeviceIdType.MESH)

    sizes = piece_sizes(block)
    starts = [sum(sizes[:p]) for p in range(len(sizes))]
    pieces = range(len(sizes))
    basis_load = pltpu.make_async_copy(basis, bbuf, load_sems.at[0])
    basis_load.start()
    loads = {}
    for p in pieces:
        for own in range(2):
            for k in range(4):
                side = core if own else 1 - core
                first = pl.multiple_of(side * half + order[k] * block + starts[p], 16)
                spot_in = own * half + 4 * starts[p] + k * sizes[p]
                load = pltpu.make_async_copy(
                    fields.at[pl.ds(first, sizes[p])], fbuf.at[pl.ds(spot_in, sizes[p])],
                    load_sems.at[1 + (p * 2 + own) * 4 + k])
                load.start()
                loads[p, own, k] = load
    basis_load.wait()

    def product(p, own):
        for k in range(4):
            loads[p, own, k].wait()
        first = own * half + 4 * starts[p]
        return jnp.dot(fbuf[first:first + 4 * sizes[p], :], bbuf[...], preferred_element_type=jnp.float32)

    started = []

    def begin(*what):
        copy = send(*what)
        copy.start()
        started.append(copy)
        return copy

    def span(p):
        return pl.ds(4 * starts[p], 4 * sizes[p])

    pair_copies, plane_copies = [], {}

    def give_piece(p):
        give[span(p), :] = product(p, 0)
        if p == 0:
            pl.semaphore_wait(barrier, 1 + 3 + lines - 1)
        pair_copies.append(begin(give.at[span(p)], take.at[span(p)], pair_send.at[p], pair_recv.at[p], partner))

    def spread_piece(p):
        pair_copies[p].wait_recv()
        mine[span(p), :] = mine[span(p), :] + take[span(p), :]
        for k in range(3):
            plane_copies[p, k] = begin(
                mine.at[pl.ds(4 * starts[p] + k * sizes[p], sizes[p])], parts.at[k, pl.ds(starts[p], sizes[p])],
                plane_send.at[p * 3 + k], plane_recv.at[p * 3 + k], plane_peers[k])

    give_piece(0)
    mine[span(0), :] = product(0, 1)
    for p in pieces[1:]:
        give_piece(p)
        spread_piece(p - 1)
        mine[span(p), :] = product(p, 1)
    spread_piece(pieces[-1])

    def rows_of(p):
        return pl.ds(starts[p], sizes[p])

    for p in pieces:
        first = 4 * starts[p] + 3 * sizes[p]
        total = mine[first:first + sizes[p], :]
        for k in (2, 1, 0):
            plane_copies[p, k].wait_recv()
            total = total + parts[k, rows_of(p), :]
        stack[line, rows_of(p), :] = total
        for step, device in enumerate(line_devices):
            slot = stack.at[line, rows_of(p)]
            begin(slot, slot, line_send.at[p * lines + step], line_recv.at[p * lines + line], device)

    def place(side, k, p):
        return out.at[pl.ds(pl.multiple_of(side * half + order[k] * block + starts[p], 8), sizes[p])]

    def forward(k, p):
        begin(place(core, k, p), place(core, k, p), final_send.at[p * 4 + k], final_recv.at[p * 4 + k], partner)

    for p in pieces:
        for step, source in enumerate(line_sources):
            slot = stack.at[source, rows_of(p)]
            send(slot, slot, line_send.at[p * lines + step], line_recv.at[p * lines + source],
                 (source * 4 + plane) * 2 + core).wait_recv()
        total = stack[0, rows_of(p), :]
        for j in range(1, lines):
            total = total + stack[j, rows_of(p), :]
        place(core, 3, p)[...] = total
        for k in range(3):
            begin(place(core, 3, p), place(core, 3, p), back_send.at[p * 3 + k], back_recv.at[p * 3 + k],
                  plane_peers[k])
        forward(3, p)
    for p in pieces:
        for k in (2, 1, 0):
            send(place(core, k, p), place(core, k, p), back_send.at[p * 3 + k], back_recv.at[p * 3 + k],
                 plane_peers[k]).wait_recv()
            forward(k, p)
    for p in pieces:
        for k in (3, 2, 1, 0):
            send(place(1 - core, k, p), place(1 - core, k, p), final_send.at[p * 4 + k],
                 final_recv.at[p * 4 + k], partner).wait_recv()
    for copy in started:
        copy.wait_send()


def summed_amplitudes(lines, fields, basis):
    rows, depth = fields.shape
    eofs = basis.shape[1]
    half, block = rows // 2, rows // 8
    pieces = len(piece_sizes(block))
    dma = pltpu.SemaphoreType.DMA
    return pl.pallas_call(
        functools.partial(amplitude_kernel, lines),
        out_shape=jax.ShapeDtypeStruct((rows, eofs), jnp.float32),
        in_specs=[pl.BlockSpec(memory_space=pltpu.HBM)] * 2,
        out_specs=pl.BlockSpec(memory_space=pltpu.VMEM),
        scratch_shapes=[
            pltpu.VMEM((rows, depth), jnp.bfloat16),
            pltpu.VMEM((depth, eofs), jnp.bfloat16),
            pltpu.VMEM((half, eofs), jnp.float32),
            pltpu.VMEM((half, eofs), jnp.float32),
            pltpu.VMEM((half, eofs), jnp.float32),
            pltpu.VMEM((3, block, eofs), jnp.float32),
            pltpu.VMEM((lines, block, eofs), jnp.float32),
            dma((1 + 8 * pieces,)), dma((pieces,)), dma((pieces,)), dma((3 * pieces,)), dma((3 * pieces,)),
            dma((lines * pieces,)), dma((lines * pieces,)), dma((3 * pieces,)), dma((3 * pieces,)),
            dma((4 * pieces,)), dma((4 * pieces,)),
        ],
        compiler_params=pltpu.CompilerParams(
            collective_id=0, has_side_effects=True, vmem_limit_bytes=VMEM_BYTES),
        cost_estimate=pl.CostEstimate(
            flops=2 * rows * depth * eofs, bytes_accessed=2 * depth * (rows + eofs), transcendentals=0),
    )(fields, basis)


def split(value, pieces):
    out = []
    for _ in range(pieces):
        part = value.astype(jnp.bfloat16)
        out.append(part)
        value = value - part.astype(jnp.float32)
    return out


def regime_kernel(seeds, amplitudes, fields, member_out, centers_out, composites, fbuf, member_buf, centers_buf,
                  composite_buf, load_sems, store_sems):
    days, eofs = amplitudes.shape
    regimes, points = composites.shape
    piece = days // CHUNKS
    loads = []
    for i in range(CHUNKS):
        load = pltpu.make_async_copy(fields.at[pl.ds(i * piece, piece)], fbuf.at[pl.ds(i * piece, piece)],
                                     load_sems.at[i])
        load.start()
        loads.append(load)

    turned = amplitudes[...].T
    with_ones = jnp.concatenate([turned, jnp.ones((16, days), jnp.float32)], axis=0)
    first, second, third = split(with_ones, 3)
    exact = jnp.concatenate([first, second, third], axis=1)
    pair = jnp.concatenate([first, second, first], axis=1)
    stores = []

    def store(src, dst):
        copy = pltpu.make_async_copy(src, dst, store_sems.at[len(stores)])
        copy.start()
        stores.append(copy)

    def member(columns):
        squares = []
        for c in range(regimes):
            offset = turned - columns[:, c:c + 1]
            squares.append(jnp.sum(offset * offset, axis=0, keepdims=True))
        mean_square = jnp.concatenate(squares, axis=0) * (1.0 / eofs) + 1e-05
        weights = 1.0 / mean_square
        return weights / jnp.sum(weights, axis=0, keepdims=True)

    positions = lax.broadcasted_iota(jnp.int32, (regimes, days), 1)
    rows = lax.broadcasted_iota(jnp.int32, (regimes, days), 0)
    chosen = jnp.zeros((regimes, days), jnp.int32)
    for c in range(regimes):
        chosen = jnp.where(rows == c, seeds[c], chosen)
    selector = (chosen == positions).astype(jnp.bfloat16)
    columns = lax.dot_general(exact, jnp.concatenate([selector] * 3, axis=1), NT,
                              preferred_element_type=jnp.float32)[:eofs]
    for sweep in range(ITERS):
        q = member(columns)
        high, low = split(q * q, 2)
        weights = jnp.concatenate([high, high, low], axis=1)
        sums = lax.dot_general(pair, weights, NT, preferred_element_type=jnp.float32)
        columns = sums[:eofs] / sums[eofs:eofs + 1]
        if sweep == ITERS - 1:
            flat = lax.dot_general(weights, pair, NT, preferred_element_type=jnp.float32)
            centers_buf[...] = flat[:, :eofs] / flat[:, eofs:eofs + 1]
            store(centers_buf, centers_out)
    final = member(columns)
    squares = final * final
    scale = 1.0 / jnp.sum(squares, axis=1, keepdims=True)
    weights_bf = squares.astype(jnp.bfloat16)
    member_buf[...] = final
    store(member_buf, member_out)
    for load in loads:
        load.wait()
    width = COLUMNS if points % COLUMNS == 0 else points
    for first in range(0, points, width):
        part = slice(first, first + width)
        composite_buf[:, part] = jnp.dot(
            weights_bf, fbuf[:, part], preferred_element_type=jnp.float32) * scale
        store(composite_buf.at[:, pl.ds(first, width)], composites.at[:, pl.ds(first, width)])
    for copy in stores:
        copy.wait()


def regimes_of(seed_days, amplitudes, fields):
    days, points = fields.shape
    eofs = amplitudes.shape[1]
    regimes = seed_days.shape[0]
    vmem = pl.BlockSpec(memory_space=pltpu.VMEM)
    hbm = pl.BlockSpec(memory_space=pltpu.HBM)
    member, centers, composites = pl.pallas_call(
        regime_kernel,
        out_shape=(
            jax.ShapeDtypeStruct((regimes, days), jnp.float32),
            jax.ShapeDtypeStruct((regimes, eofs), jnp.float32),
            jax.ShapeDtypeStruct((regimes, points), jnp.float32),
        ),
        in_specs=[pl.BlockSpec(memory_space=pltpu.SMEM), vmem, hbm],
        out_specs=(hbm, hbm, hbm),
        scratch_shapes=[
            pltpu.VMEM((days, points), jnp.bfloat16),
            pltpu.VMEM((regimes, days), jnp.float32),
            pltpu.VMEM((regimes, eofs), jnp.float32),
            pltpu.VMEM((regimes, points), jnp.float32),
            pltpu.SemaphoreType.DMA((CHUNKS,)),
            pltpu.SemaphoreType.DMA((2 + max(1, points // COLUMNS),)),
        ],
        compiler_params=pltpu.CompilerParams(vmem_limit_bytes=VMEM_BYTES),
        cost_estimate=pl.CostEstimate(
            flops=2 * regimes * days * points, bytes_accessed=2 * days * points, transcendentals=0),
    )(seed_days, amplitudes, fields)
    return member.T, centers, composites


def on_device(mesh, fields, eof_basis, seed_days):
    n = mesh.shape["grid"]
    day_rows = fields.shape[0]
    if n % 8 == 0 and n > 8 and day_rows % 128 == 0:
        amplitudes = summed_amplitudes(n // 8, fields, eof_basis)
    else:
        partial_value = jnp.dot(fields, eof_basis, preferred_element_type=jnp.float32)
        amplitudes = lax.psum(partial_value, "grid")
    if mesh.shape["day"] == 1 and day_rows % 128 == 0 and eof_basis.shape[1] % 128 == 0:
        return regimes_of(seed_days, amplitudes, fields)
    first = lax.axis_index("day") * day_rows
    centers = lax.psum(seed_terms(seed_days, first, amplitudes), "day")
    for sweep in range(ITERS):
        numerator, denominator = lax.psum(regime_terms(amplitudes, centers), "day")
        centers = numerator / denominator[:, None]
    member_all = member_of(amplitudes, centers)
    squares = member_all * member_all
    weights_bf = squares.astype(jnp.bfloat16)
    weighted = jnp.dot(weights_bf.T, fields, preferred_element_type=jnp.float32)
    totals, weight_sums = lax.psum((weighted, jnp.sum(squares, axis=0)), "day")
    return (member_all, centers, totals / weight_sums[:, None])


def solution(mesh):
    placed = (P("day", "grid"), P("grid", None), P())
    return jax.shard_map(
        functools.partial(on_device, mesh),
        mesh=mesh,
        in_specs=placed,
        out_specs=(P("day", None), P(), P(None, "grid")),
        check_vma=False,
    )
```

```python
import functools

import jax
import jax.numpy as jnp
from jax import lax
from jax.experimental import pallas as pl
from jax.experimental.pallas import tpu as pltpu
from jax.sharding import PartitionSpec as P

ITERS = 3
CHUNKS = 2
VMEM_BYTES = 53 * 1024 * 1024
COLUMNS = 1024
NT = (((1,), (1,)), ((), ()))


def member_of(amplitudes, centers):
    offsets = amplitudes[:, None, :] - centers[None, :, :]
    mean_square = jnp.mean(offsets * offsets, axis=2) + 1e-05
    weights = 1.0 / mean_square
    return weights / jnp.sum(weights, axis=1, keepdims=True)


def seed_terms(seed_days, first, amplitudes):
    positions = first + jnp.arange(amplitudes.shape[0], dtype=jnp.int32)
    selector = (seed_days[:, None] == positions[None, :]).astype(jnp.float32)
    return jnp.dot(selector, amplitudes, precision=lax.Precision.HIGHEST)


def regime_terms(amplitudes, centers):
    member = member_of(amplitudes, centers)
    squared = member * member
    numerator = jnp.dot(squared.T, amplitudes, precision=lax.Precision.HIGHEST)
    return (numerator, jnp.sum(squared, axis=0))


def piece_sizes(block):
    return [16] * (block // 16)


def amplitude_kernel(lines, fields, basis, out, fbuf, bbuf, mine, parts, stack, load_sems,
                     plane_send, plane_recv, line_send, line_recv, back_send, back_recv):
    rows = out.shape[0]
    block = rows // 8
    me = lax.axis_index("grid")
    core = lax.rem(me, 2)
    px = lax.rem(me // 2, 2)
    py = lax.rem(me // 4, 2)
    line = me // 8
    flips = [(1, 1, 0), (1, 1, 1), (1, 0, 0), (1, 0, 1), (0, 1, 0), (0, 1, 1), (0, 0, 1), (0, 0, 0)]
    order = []
    for fy, fx, fc in flips:
        y = 1 - py if fy else py
        x = 1 - px if fx else px
        c = 1 - core if fc else core
        order.append((y * 2 + x) * 2 + c)
    own = order[7]

    def send(src, dst, send_sem, recv_sem, device):
        return pltpu.make_async_remote_copy(
            src_ref=src, dst_ref=dst, send_sem=send_sem, recv_sem=recv_sem,
            device_id={"grid": device}, device_id_type=pl.DeviceIdType.MESH)

    plane_peers = [line * 8 + position for position in order[:7]]
    line_steps = sorted(range(1, lines), key=lambda step: -min(step, lines - step))
    line_devices = [lax.rem(line + step, lines) * 8 + own for step in line_steps]
    line_sources = [lax.rem(line + lines - step, lines) for step in line_steps]

    barrier = pltpu.get_barrier_semaphore()
    for device in line_devices + plane_peers:
        pl.semaphore_signal(barrier, inc=1, device_id={"grid": device}, device_id_type=pl.DeviceIdType.MESH)

    sizes = piece_sizes(block)
    starts = [sum(sizes[:p]) for p in range(len(sizes))]
    pieces = range(len(sizes))
    basis_load = pltpu.make_async_copy(basis, bbuf, load_sems.at[0])
    basis_load.start()
    loads = {}
    for p in pieces:
        for k in range(8):
            first = pl.multiple_of(order[k] * block + starts[p], 16)
            load = pltpu.make_async_copy(
                fields.at[pl.ds(first, sizes[p])], fbuf.at[pl.ds(8 * starts[p] + k * sizes[p], sizes[p])],
                load_sems.at[1 + p * 8 + k])
            load.start()
            loads[p, k] = load

    started = []

    def begin(*what):
        copy = send(*what)
        copy.start()
        started.append(copy)
        return copy

    def rows_of(p):
        return pl.ds(starts[p], sizes[p])

    basis_load.wait()
    plane_copies = {}
    for p in pieces:
        for k in range(8):
            loads[p, k].wait()
        span = slice(8 * starts[p], 8 * (starts[p] + sizes[p]))
        mine[span, :] = jnp.dot(fbuf[span, :], bbuf[...], preferred_element_type=jnp.float32)
        if p == 0:
            pl.semaphore_wait(barrier, 7 + lines - 1)
        for k in range(7):
            plane_copies[p, k] = begin(
                mine.at[pl.ds(8 * starts[p] + k * sizes[p], sizes[p])], parts.at[k, rows_of(p)],
                plane_send.at[p * 7 + k], plane_recv.at[p * 7 + k], plane_peers[k])

    for p in pieces:
        first = 8 * starts[p] + 7 * sizes[p]
        total = mine[first:first + sizes[p], :]
        for k in reversed(range(7)):
            plane_copies[p, k].wait_recv()
            total = total + parts[k, rows_of(p), :]
        stack[line, rows_of(p), :] = total
        slot = stack.at[line, rows_of(p)]
        for step, device in enumerate(line_devices):
            begin(slot, slot, line_send.at[p * lines + step], line_recv.at[p * lines + line], device)

    def place(k, p):
        return out.at[pl.ds(pl.multiple_of(order[k] * block + starts[p], 8), sizes[p])]

    for p in pieces:
        for step, source in enumerate(line_sources):
            slot = stack.at[source, rows_of(p)]
            send(slot, slot, line_send.at[p * lines + step], line_recv.at[p * lines + source],
                 source * 8 + own).wait_recv()
        total = stack[0, rows_of(p), :]
        for j in range(1, lines):
            total = total + stack[j, rows_of(p), :]
        place(7, p)[...] = total
        for k in range(7):
            begin(place(7, p), place(7, p), back_send.at[p * 7 + k], back_recv.at[p * 7 + k], plane_peers[k])
    for p in pieces:
        for k in reversed(range(7)):
            send(place(k, p), place(k, p), back_send.at[p * 7 + k], back_recv.at[p * 7 + k],
                 plane_peers[k]).wait_recv()
    for copy in started:
        copy.wait_send()


def summed_amplitudes(lines, fields, basis):
    rows, depth = fields.shape
    eofs = basis.shape[1]
    block = rows // 8
    pieces = len(piece_sizes(block))
    dma = pltpu.SemaphoreType.DMA
    return pl.pallas_call(
        functools.partial(amplitude_kernel, lines),
        out_shape=jax.ShapeDtypeStruct((rows, eofs), jnp.float32),
        in_specs=[pl.BlockSpec(memory_space=pltpu.HBM)] * 2,
        out_specs=pl.BlockSpec(memory_space=pltpu.VMEM),
        scratch_shapes=[
            pltpu.VMEM((rows, depth), jnp.bfloat16),
            pltpu.VMEM((depth, eofs), jnp.bfloat16),
            pltpu.VMEM((rows, eofs), jnp.float32),
            pltpu.VMEM((7, block, eofs), jnp.float32),
            pltpu.VMEM((lines, block, eofs), jnp.float32),
            dma((1 + 8 * pieces,)), dma((7 * pieces,)), dma((7 * pieces,)),
            dma((lines * pieces,)), dma((lines * pieces,)), dma((7 * pieces,)), dma((7 * pieces,)),
        ],
        compiler_params=pltpu.CompilerParams(
            collective_id=0, has_side_effects=True, vmem_limit_bytes=VMEM_BYTES),
        cost_estimate=pl.CostEstimate(
            flops=2 * rows * depth * eofs, bytes_accessed=2 * depth * (rows + eofs), transcendentals=0),
    )(fields, basis)


def split(value, pieces):
    out = []
    for _ in range(pieces):
        part = value.astype(jnp.bfloat16)
        out.append(part)
        value = value - part.astype(jnp.float32)
    return out


def regime_kernel(seeds, amplitudes, fields, member_out, centers_out, composites, fbuf, member_buf, centers_buf,
                  composite_buf, load_sems, store_sems):
    days, eofs = amplitudes.shape
    regimes, points = composites.shape
    piece = days // CHUNKS
    loads = []
    for i in range(CHUNKS):
        load = pltpu.make_async_copy(fields.at[pl.ds(i * piece, piece)], fbuf.at[pl.ds(i * piece, piece)],
                                     load_sems.at[i])
        load.start()
        loads.append(load)

    turned = amplitudes[...].T
    with_ones = jnp.concatenate([turned, jnp.ones((16, days), jnp.float32)], axis=0)
    first, second, third = split(with_ones, 3)
    exact = jnp.concatenate([first, second, third], axis=1)
    pair = jnp.concatenate([first, second, first], axis=1)
    stores = []

    def store(src, dst):
        copy = pltpu.make_async_copy(src, dst, store_sems.at[len(stores)])
        copy.start()
        stores.append(copy)

    def member(columns):
        squares = []
        for c in range(regimes):
            offset = turned - columns[:, c:c + 1]
            squares.append(jnp.sum(offset * offset, axis=0, keepdims=True))
        mean_square = jnp.concatenate(squares, axis=0) * (1.0 / eofs) + 1e-05
        weights = 1.0 / mean_square
        return weights / jnp.sum(weights, axis=0, keepdims=True)

    positions = lax.broadcasted_iota(jnp.int32, (regimes, days), 1)
    rows = lax.broadcasted_iota(jnp.int32, (regimes, days), 0)
    chosen = jnp.zeros((regimes, days), jnp.int32)
    for c in range(regimes):
        chosen = jnp.where(rows == c, seeds[c], chosen)
    selector = (chosen == positions).astype(jnp.bfloat16)
    columns = lax.dot_general(exact, jnp.concatenate([selector] * 3, axis=1), NT,
                              preferred_element_type=jnp.float32)[:eofs]
    for sweep in range(ITERS):
        q = member(columns)
        high, low = split(q * q, 2)
        weights = jnp.concatenate([high, high, low], axis=1)
        sums = lax.dot_general(pair, weights, NT, preferred_element_type=jnp.float32)
        columns = sums[:eofs] / sums[eofs:eofs + 1]
        if sweep == ITERS - 1:
            flat = lax.dot_general(weights, pair, NT, preferred_element_type=jnp.float32)
            centers_buf[...] = flat[:, :eofs] / flat[:, eofs:eofs + 1]
            store(centers_buf, centers_out)
    final = member(columns)
    squares = final * final
    scale = 1.0 / jnp.sum(squares, axis=1, keepdims=True)
    weights_bf = squares.astype(jnp.bfloat16)
    member_buf[...] = final
    store(member_buf, member_out)
    for load in loads:
        load.wait()
    width = COLUMNS if points % COLUMNS == 0 else points
    for first in range(0, points, width):
        part = slice(first, first + width)
        composite_buf[:, part] = jnp.dot(
            weights_bf, fbuf[:, part], preferred_element_type=jnp.float32) * scale
        store(composite_buf.at[:, pl.ds(first, width)], composites.at[:, pl.ds(first, width)])
    for copy in stores:
        copy.wait()


def regimes_of(seed_days, amplitudes, fields):
    days, points = fields.shape
    eofs = amplitudes.shape[1]
    regimes = seed_days.shape[0]
    vmem = pl.BlockSpec(memory_space=pltpu.VMEM)
    hbm = pl.BlockSpec(memory_space=pltpu.HBM)
    member, centers, composites = pl.pallas_call(
        regime_kernel,
        out_shape=(
            jax.ShapeDtypeStruct((regimes, days), jnp.float32),
            jax.ShapeDtypeStruct((regimes, eofs), jnp.float32),
            jax.ShapeDtypeStruct((regimes, points), jnp.float32),
        ),
        in_specs=[pl.BlockSpec(memory_space=pltpu.SMEM), vmem, hbm],
        out_specs=(hbm, hbm, hbm),
        scratch_shapes=[
            pltpu.VMEM((days, points), jnp.bfloat16),
            pltpu.VMEM((regimes, days), jnp.float32),
            pltpu.VMEM((regimes, eofs), jnp.float32),
            pltpu.VMEM((regimes, points), jnp.float32),
            pltpu.SemaphoreType.DMA((CHUNKS,)),
            pltpu.SemaphoreType.DMA((2 + max(1, points // COLUMNS),)),
        ],
        compiler_params=pltpu.CompilerParams(vmem_limit_bytes=VMEM_BYTES),
        cost_estimate=pl.CostEstimate(
            flops=2 * regimes * days * points, bytes_accessed=2 * days * points, transcendentals=0),
    )(seed_days, amplitudes, fields)
    return member.T, centers, composites


def on_device(mesh, fields, eof_basis, seed_days):
    n = mesh.shape["grid"]
    day_rows = fields.shape[0]
    if n % 8 == 0 and n > 8 and day_rows % 128 == 0:
        amplitudes = summed_amplitudes(n // 8, fields, eof_basis)
    else:
        partial_value = jnp.dot(fields, eof_basis, preferred_element_type=jnp.float32)
        amplitudes = lax.psum(partial_value, "grid")
    if mesh.shape["day"] == 1 and day_rows % 128 == 0 and eof_basis.shape[1] % 128 == 0:
        return regimes_of(seed_days, amplitudes, fields)
    first = lax.axis_index("day") * day_rows
    centers = lax.psum(seed_terms(seed_days, first, amplitudes), "day")
    for sweep in range(ITERS):
        numerator, denominator = lax.psum(regime_terms(amplitudes, centers), "day")
        centers = numerator / denominator[:, None]
    member_all = member_of(amplitudes, centers)
    squares = member_all * member_all
    weights_bf = squares.astype(jnp.bfloat16)
    weighted = jnp.dot(weights_bf.T, fields, preferred_element_type=jnp.float32)
    totals, weight_sums = lax.psum((weighted, jnp.sum(squares, axis=0)), "day")
    return (member_all, centers, totals / weight_sums[:, None])


def solution(mesh):
    placed = (P("day", "grid"), P("grid", None), P())
    return jax.shard_map(
        functools.partial(on_device, mesh),
        mesh=mesh,
        in_specs=placed,
        out_specs=(P("day", None), P(), P(None, "grid")),
        check_vma=False,
    )
```

```python
import functools

import jax
import jax.numpy as jnp
from jax import lax
from jax.experimental import pallas as pl
from jax.experimental.pallas import tpu as pltpu
from jax.sharding import PartitionSpec as P

ITERS = 3
CHUNKS = 2
VMEM_BYTES = 53 * 1024 * 1024
COLUMNS = 1024
BASIS_COPIES = 4
NT = (((1,), (1,)), ((), ()))


def member_of(amplitudes, centers):
    offsets = amplitudes[:, None, :] - centers[None, :, :]
    mean_square = jnp.mean(offsets * offsets, axis=2) + 1e-05
    weights = 1.0 / mean_square
    return weights / jnp.sum(weights, axis=1, keepdims=True)


def seed_terms(seed_days, first, amplitudes):
    positions = first + jnp.arange(amplitudes.shape[0], dtype=jnp.int32)
    selector = (seed_days[:, None] == positions[None, :]).astype(jnp.float32)
    return jnp.dot(selector, amplitudes, precision=lax.Precision.HIGHEST)


def regime_terms(amplitudes, centers):
    member = member_of(amplitudes, centers)
    squared = member * member
    numerator = jnp.dot(squared.T, amplitudes, precision=lax.Precision.HIGHEST)
    return (numerator, jnp.sum(squared, axis=0))


def piece_sizes(block):
    return [16] * (block // 16)


def amplitude_kernel(lines, fields, basis, out, fbuf, bbuf, mine, take, parts, stack, load_sems,
                     pair_send, pair_recv, plane_send, plane_recv, line_send, line_recv, back_send, back_recv):
    rows = out.shape[0]
    block = rows // 8
    me = lax.axis_index("grid")
    core = lax.rem(me, 2)
    px = lax.rem(me // 2, 2)
    py = lax.rem(me // 4, 2)
    line = me // 8
    flips = [(1, 1, 1), (1, 0, 1), (0, 1, 1), (0, 0, 1), (1, 1, 0), (1, 0, 0), (0, 1, 0), (0, 0, 0)]
    order = []
    for fy, fx, fc in flips:
        y = 1 - py if fy else py
        x = 1 - px if fx else px
        c = 1 - core if fc else core
        order.append((y * 2 + x) * 2 + c)
    own = order[7]

    def send(src, dst, send_sem, recv_sem, device):
        return pltpu.make_async_remote_copy(
            src_ref=src, dst_ref=dst, send_sem=send_sem, recv_sem=recv_sem,
            device_id={"grid": device}, device_id_type=pl.DeviceIdType.MESH)

    plane_peers = [line * 8 + position for position in order[:7]]
    line_steps = sorted(range(1, lines), key=lambda step: -min(step, lines - step))
    line_devices = [lax.rem(line + step, lines) * 8 + own for step in line_steps]
    line_sources = [lax.rem(line + lines - step, lines) for step in line_steps]

    barrier = pltpu.get_barrier_semaphore()
    for device in line_devices + plane_peers:
        pl.semaphore_signal(barrier, inc=1, device_id={"grid": device}, device_id_type=pl.DeviceIdType.MESH)

    sizes = piece_sizes(block)
    starts = [sum(sizes[:p]) for p in range(len(sizes))]
    pieces = range(len(sizes))
    depth = basis.shape[0] // BASIS_COPIES
    basis_loads = []
    for i in range(BASIS_COPIES):
        part = pl.ds(i * depth, depth)
        load = pltpu.make_async_copy(basis.at[part], bbuf.at[part], load_sems.at[i])
        load.start()
        basis_loads.append(load)
    loads = {}
    for p in pieces:
        for k in range(8):
            first = pl.multiple_of(order[k] * block + starts[p], 16)
            load = pltpu.make_async_copy(
                fields.at[pl.ds(first, sizes[p])], fbuf.at[pl.ds(8 * starts[p] + k * sizes[p], sizes[p])],
                load_sems.at[BASIS_COPIES + p * 8 + k])
            load.start()
            loads[p, k] = load

    started = []

    def begin(*what):
        copy = send(*what)
        copy.start()
        started.append(copy)
        return copy

    def rows_of(p):
        return pl.ds(starts[p], sizes[p])

    for load in basis_loads:
        load.wait()
    pair_copies, plane_copies = [], {}

    def spread_piece(p):
        first = 8 * starts[p] + 4 * sizes[p]
        pair_copies[p].wait_recv()
        mine[first:first + 4 * sizes[p], :] = (
            mine[first:first + 4 * sizes[p], :] + take[4 * starts[p]:4 * (starts[p] + sizes[p]), :])
        for k in range(3):
            plane_copies[p, k] = begin(
                mine.at[pl.ds(first + k * sizes[p], sizes[p])], parts.at[k, rows_of(p)],
                plane_send.at[p * 3 + k], plane_recv.at[p * 3 + k], plane_peers[4 + k])

    for p in pieces:
        for k in range(8):
            loads[p, k].wait()
        span = slice(8 * starts[p], 8 * (starts[p] + sizes[p]))
        mine[span, :] = jnp.dot(fbuf[span, :], bbuf[...], preferred_element_type=jnp.float32)
        if p == 0:
            pl.semaphore_wait(barrier, 7 + lines - 1)
        pair_copies.append(begin(
            mine.at[pl.ds(8 * starts[p], 4 * sizes[p])], take.at[pl.ds(4 * starts[p], 4 * sizes[p])],
            pair_send.at[p], pair_recv.at[p], plane_peers[3]))
        if p > 0:
            spread_piece(p - 1)
    spread_piece(pieces[-1])

    for p in pieces:
        first = 8 * starts[p] + 7 * sizes[p]
        total = mine[first:first + sizes[p], :]
        for k in (2, 1, 0):
            plane_copies[p, k].wait_recv()
            total = total + parts[k, rows_of(p), :]
        stack[line, rows_of(p), :] = total
        slot = stack.at[line, rows_of(p)]
        for step, device in enumerate(line_devices):
            begin(slot, slot, line_send.at[p * lines + step], line_recv.at[p * lines + line], device)

    back_order = (0, 4, 1, 5, 2, 6, 3)

    def place(k, p):
        return out.at[pl.ds(pl.multiple_of(order[k] * block + starts[p], 8), sizes[p])]

    for p in pieces:
        for step, source in enumerate(line_sources):
            slot = stack.at[source, rows_of(p)]
            send(slot, slot, line_send.at[p * lines + step], line_recv.at[p * lines + source],
                 source * 8 + own).wait_recv()
        total = stack[0, rows_of(p), :]
        for j in range(1, lines):
            total = total + stack[j, rows_of(p), :]
        place(7, p)[...] = total
        for k in back_order:
            begin(place(7, p), place(7, p), back_send.at[p * 7 + k], back_recv.at[p * 7 + k], plane_peers[k])
    for p in pieces:
        for k in reversed(back_order):
            send(place(k, p), place(k, p), back_send.at[p * 7 + k], back_recv.at[p * 7 + k],
                 plane_peers[k]).wait_recv()
    for copy in started:
        copy.wait_send()


def summed_amplitudes(lines, fields, basis):
    rows, depth = fields.shape
    eofs = basis.shape[1]
    block = rows // 8
    pieces = len(piece_sizes(block))
    dma = pltpu.SemaphoreType.DMA
    return pl.pallas_call(
        functools.partial(amplitude_kernel, lines),
        out_shape=jax.ShapeDtypeStruct((rows, eofs), jnp.float32),
        in_specs=[pl.BlockSpec(memory_space=pltpu.HBM)] * 2,
        out_specs=pl.BlockSpec(memory_space=pltpu.VMEM),
        scratch_shapes=[
            pltpu.VMEM((rows, depth), jnp.bfloat16),
            pltpu.VMEM((depth, eofs), jnp.bfloat16),
            pltpu.VMEM((rows, eofs), jnp.float32),
            pltpu.VMEM((rows // 2, eofs), jnp.float32),
            pltpu.VMEM((3, block, eofs), jnp.float32),
            pltpu.VMEM((lines, block, eofs), jnp.float32),
            dma((BASIS_COPIES + 8 * pieces,)), dma((pieces,)), dma((pieces,)), dma((3 * pieces,)), dma((3 * pieces,)),
            dma((lines * pieces,)), dma((lines * pieces,)), dma((7 * pieces,)), dma((7 * pieces,)),
        ],
        compiler_params=pltpu.CompilerParams(
            collective_id=0, has_side_effects=True, vmem_limit_bytes=VMEM_BYTES),
        cost_estimate=pl.CostEstimate(
            flops=2 * rows * depth * eofs, bytes_accessed=2 * depth * (rows + eofs), transcendentals=0),
    )(fields, basis)


def split(value, pieces):
    out = []
    for _ in range(pieces):
        part = value.astype(jnp.bfloat16)
        out.append(part)
        value = value - part.astype(jnp.float32)
    return out


def regime_kernel(seeds, amplitudes, fields, member_out, centers_out, composites, fbuf, member_buf, centers_buf,
                  composite_buf, load_sems, store_sems):
    days, eofs = amplitudes.shape
    regimes, points = composites.shape
    piece = days // CHUNKS
    loads = []
    for i in range(CHUNKS):
        load = pltpu.make_async_copy(fields.at[pl.ds(i * piece, piece)], fbuf.at[pl.ds(i * piece, piece)],
                                     load_sems.at[i])
        load.start()
        loads.append(load)

    turned = amplitudes[...].T
    with_ones = jnp.concatenate([turned, jnp.ones((16, days), jnp.float32)], axis=0)
    first, second, third = split(with_ones, 3)
    exact = jnp.concatenate([first, second, third], axis=1)
    pair = jnp.concatenate([first, second, first], axis=1)
    stores = []

    def store(src, dst):
        copy = pltpu.make_async_copy(src, dst, store_sems.at[len(stores)])
        copy.start()
        stores.append(copy)

    def member(columns):
        squares = []
        for c in range(regimes):
            offset = turned - columns[:, c:c + 1]
            squares.append(jnp.sum(offset * offset, axis=0, keepdims=True))
        mean_square = jnp.concatenate(squares, axis=0) * (1.0 / eofs) + 1e-05
        weights = 1.0 / mean_square
        return weights / jnp.sum(weights, axis=0, keepdims=True)

    positions = lax.broadcasted_iota(jnp.int32, (regimes, days), 1)
    rows = lax.broadcasted_iota(jnp.int32, (regimes, days), 0)
    chosen = jnp.zeros((regimes, days), jnp.int32)
    for c in range(regimes):
        chosen = jnp.where(rows == c, seeds[c], chosen)
    selector = (chosen == positions).astype(jnp.bfloat16)
    columns = lax.dot_general(exact, jnp.concatenate([selector] * 3, axis=1), NT,
                              preferred_element_type=jnp.float32)[:eofs]
    for sweep in range(ITERS):
        q = member(columns)
        high, low = split(q * q, 2)
        weights = jnp.concatenate([high, high, low], axis=1)
        sums = lax.dot_general(pair, weights, NT, preferred_element_type=jnp.float32)
        columns = sums[:eofs] / sums[eofs:eofs + 1]
        if sweep == ITERS - 1:
            flat = lax.dot_general(weights, pair, NT, preferred_element_type=jnp.float32)
            centers_buf[...] = flat[:, :eofs] / flat[:, eofs:eofs + 1]
            store(centers_buf, centers_out)
    final = member(columns)
    squares = final * final
    scale = 1.0 / jnp.sum(squares, axis=1, keepdims=True)
    weights_bf = squares.astype(jnp.bfloat16)
    member_buf[...] = final
    store(member_buf, member_out)
    for load in loads:
        load.wait()
    width = COLUMNS if points % COLUMNS == 0 else points
    for first in range(0, points, width):
        part = slice(first, first + width)
        composite_buf[:, part] = jnp.dot(
            weights_bf, fbuf[:, part], preferred_element_type=jnp.float32) * scale
        store(composite_buf.at[:, pl.ds(first, width)], composites.at[:, pl.ds(first, width)])
    for copy in stores:
        copy.wait()


def regimes_of(seed_days, amplitudes, fields):
    days, points = fields.shape
    eofs = amplitudes.shape[1]
    regimes = seed_days.shape[0]
    vmem = pl.BlockSpec(memory_space=pltpu.VMEM)
    hbm = pl.BlockSpec(memory_space=pltpu.HBM)
    member, centers, composites = pl.pallas_call(
        regime_kernel,
        out_shape=(
            jax.ShapeDtypeStruct((regimes, days), jnp.float32),
            jax.ShapeDtypeStruct((regimes, eofs), jnp.float32),
            jax.ShapeDtypeStruct((regimes, points), jnp.float32),
        ),
        in_specs=[pl.BlockSpec(memory_space=pltpu.SMEM), vmem, hbm],
        out_specs=(hbm, hbm, hbm),
        scratch_shapes=[
            pltpu.VMEM((days, points), jnp.bfloat16),
            pltpu.VMEM((regimes, days), jnp.float32),
            pltpu.VMEM((regimes, eofs), jnp.float32),
            pltpu.VMEM((regimes, points), jnp.float32),
            pltpu.SemaphoreType.DMA((CHUNKS,)),
            pltpu.SemaphoreType.DMA((2 + max(1, points // COLUMNS),)),
        ],
        compiler_params=pltpu.CompilerParams(vmem_limit_bytes=VMEM_BYTES),
        cost_estimate=pl.CostEstimate(
            flops=2 * regimes * days * points, bytes_accessed=2 * days * points, transcendentals=0),
    )(seed_days, amplitudes, fields)
    return member.T, centers, composites


def on_device(mesh, fields, eof_basis, seed_days):
    n = mesh.shape["grid"]
    day_rows = fields.shape[0]
    if n % 8 == 0 and n > 8 and day_rows % 128 == 0 and eof_basis.shape[0] % (16 * BASIS_COPIES) == 0:
        amplitudes = summed_amplitudes(n // 8, fields, eof_basis)
    else:
        partial_value = jnp.dot(fields, eof_basis, preferred_element_type=jnp.float32)
        amplitudes = lax.psum(partial_value, "grid")
    if mesh.shape["day"] == 1 and day_rows % 128 == 0 and eof_basis.shape[1] % 128 == 0:
        return regimes_of(seed_days, amplitudes, fields)
    first = lax.axis_index("day") * day_rows
    centers = lax.psum(seed_terms(seed_days, first, amplitudes), "day")
    for sweep in range(ITERS):
        numerator, denominator = lax.psum(regime_terms(amplitudes, centers), "day")
        centers = numerator / denominator[:, None]
    member_all = member_of(amplitudes, centers)
    squares = member_all * member_all
    weights_bf = squares.astype(jnp.bfloat16)
    weighted = jnp.dot(weights_bf.T, fields, preferred_element_type=jnp.float32)
    totals, weight_sums = lax.psum((weighted, jnp.sum(squares, axis=0)), "day")
    return (member_all, centers, totals / weight_sums[:, None])


def solution(mesh):
    placed = (P("day", "grid"), P("grid", None), P())
    return jax.shard_map(
        functools.partial(on_device, mesh),
        mesh=mesh,
        in_specs=placed,
        out_specs=(P("day", None), P(), P(None, "grid")),
        check_vma=False,
    )
```

```python
import functools

import jax
import jax.numpy as jnp
from jax import lax
from jax.experimental import pallas as pl
from jax.experimental.pallas import tpu as pltpu
from jax.sharding import PartitionSpec as P

ITERS = 3
CHUNKS = 2
VMEM_BYTES = 53 * 1024 * 1024
COLUMNS = 1024
NT = (((1,), (1,)), ((), ()))


def member_of(amplitudes, centers):
    offsets = amplitudes[:, None, :] - centers[None, :, :]
    mean_square = jnp.mean(offsets * offsets, axis=2) + 1e-05
    weights = 1.0 / mean_square
    return weights / jnp.sum(weights, axis=1, keepdims=True)


def seed_terms(seed_days, first, amplitudes):
    positions = first + jnp.arange(amplitudes.shape[0], dtype=jnp.int32)
    selector = (seed_days[:, None] == positions[None, :]).astype(jnp.float32)
    return jnp.dot(selector, amplitudes, precision=lax.Precision.HIGHEST)


def regime_terms(amplitudes, centers):
    member = member_of(amplitudes, centers)
    squared = member * member
    numerator = jnp.dot(squared.T, amplitudes, precision=lax.Precision.HIGHEST)
    return (numerator, jnp.sum(squared, axis=0))


def piece_sizes(block):
    return [block - 16, 16] if block > 16 else [block]


def amplitude_kernel(lines, fields, basis, out, fbuf, bbuf, mine, parts, stack, load_sems,
                     plane_send, plane_recv, line_send, line_recv, back_send, back_recv):
    rows = out.shape[0]
    block = rows // 8
    me = lax.axis_index("grid")
    core = lax.rem(me, 2)
    px = lax.rem(me // 2, 2)
    py = lax.rem(me // 4, 2)
    line = me // 8
    flips = [(1, 1, 0), (1, 1, 1), (1, 0, 0), (1, 0, 1), (0, 1, 0), (0, 1, 1), (0, 0, 1), (0, 0, 0)]
    order = []
    for fy, fx, fc in flips:
        y = 1 - py if fy else py
        x = 1 - px if fx else px
        c = 1 - core if fc else core
        order.append((y * 2 + x) * 2 + c)
    own = order[7]

    def send(src, dst, send_sem, recv_sem, device):
        return pltpu.make_async_remote_copy(
            src_ref=src, dst_ref=dst, send_sem=send_sem, recv_sem=recv_sem,
            device_id={"grid": device}, device_id_type=pl.DeviceIdType.MESH)

    plane_peers = [line * 8 + position for position in order[:7]]
    line_steps = sorted(range(1, lines), key=lambda step: -min(step, lines - step))
    line_devices = [lax.rem(line + step, lines) * 8 + own for step in line_steps]
    line_sources = [lax.rem(line + lines - step, lines) for step in line_steps]

    barrier = pltpu.get_barrier_semaphore()
    for device in line_devices + plane_peers:
        pl.semaphore_signal(barrier, inc=1, device_id={"grid": device}, device_id_type=pl.DeviceIdType.MESH)

    sizes = piece_sizes(block)
    starts = [sum(sizes[:p]) for p in range(len(sizes))]
    pieces = range(len(sizes))
    basis_load = pltpu.make_async_copy(basis, bbuf, load_sems.at[0])
    basis_load.start()
    loads = {}
    for p in pieces:
        for k in range(8):
            first = pl.multiple_of(order[k] * block + starts[p], 16)
            load = pltpu.make_async_copy(
                fields.at[pl.ds(first, sizes[p])], fbuf.at[pl.ds(8 * starts[p] + k * sizes[p], sizes[p])],
                load_sems.at[1 + p * 8 + k])
            load.start()
            loads[p, k] = load

    started = []

    def begin(*what):
        copy = send(*what)
        copy.start()
        started.append(copy)
        return copy

    def rows_of(p):
        return pl.ds(starts[p], sizes[p])

    basis_load.wait()
    plane_copies = {}
    for p in pieces:
        for k in range(8):
            loads[p, k].wait()
        span = slice(8 * starts[p], 8 * (starts[p] + sizes[p]))
        mine[span, :] = jnp.dot(fbuf[span, :], bbuf[...], preferred_element_type=jnp.float32)
        if p == 0:
            pl.semaphore_wait(barrier, 7 + lines - 1)
        for k in range(7):
            plane_copies[p, k] = begin(
                mine.at[pl.ds(8 * starts[p] + k * sizes[p], sizes[p])], parts.at[k, rows_of(p)],
                plane_send.at[p * 7 + k], plane_recv.at[p * 7 + k], plane_peers[k])

    for p in pieces:
        first = 8 * starts[p] + 7 * sizes[p]
        total = mine[first:first + sizes[p], :]
        for k in reversed(range(7)):
            plane_copies[p, k].wait_recv()
            total = total + parts[k, rows_of(p), :]
        stack[line, rows_of(p), :] = total
        slot = stack.at[line, rows_of(p)]
        for step, device in enumerate(line_devices):
            begin(slot, slot, line_send.at[p * lines + step], line_recv.at[p * lines + line], device)

    def drain():
        while started:
            started.pop().wait_send()

    def place(k, p):
        return out.at[pl.ds(pl.multiple_of(order[k] * block + starts[p], 8), sizes[p])]

    line_copies = started[-len(pieces) * (lines - 1):]
    del started[-len(pieces) * (lines - 1):]
    drain()
    for p in pieces:
        for step, source in enumerate(line_sources):
            slot = stack.at[source, rows_of(p)]
            send(slot, slot, line_send.at[p * lines + step], line_recv.at[p * lines + source],
                 source * 8 + own).wait_recv()
        total = stack[0, rows_of(p), :]
        for j in range(1, lines):
            total = total + stack[j, rows_of(p), :]
        place(7, p)[...] = total
        for k in range(7):
            begin(place(7, p), place(7, p), back_send.at[p * 7 + k], back_recv.at[p * 7 + k], plane_peers[k])
    for copy in line_copies:
        copy.wait_send()
    for p in pieces:
        for k in reversed(range(7)):
            send(place(k, p), place(k, p), back_send.at[p * 7 + k], back_recv.at[p * 7 + k],
                 plane_peers[k]).wait_recv()
    drain()


def summed_amplitudes(lines, fields, basis):
    rows, depth = fields.shape
    eofs = basis.shape[1]
    block = rows // 8
    pieces = len(piece_sizes(block))
    dma = pltpu.SemaphoreType.DMA
    return pl.pallas_call(
        functools.partial(amplitude_kernel, lines),
        out_shape=jax.ShapeDtypeStruct((rows, eofs), jnp.float32),
        in_specs=[pl.BlockSpec(memory_space=pltpu.HBM)] * 2,
        out_specs=pl.BlockSpec(memory_space=pltpu.VMEM),
        scratch_shapes=[
            pltpu.VMEM((rows, depth), jnp.bfloat16),
            pltpu.VMEM((depth, eofs), jnp.bfloat16),
            pltpu.VMEM((rows, eofs), jnp.float32),
            pltpu.VMEM((7, block, eofs), jnp.float32),
            pltpu.VMEM((lines, block, eofs), jnp.float32),
            dma((1 + 8 * pieces,)), dma((7 * pieces,)), dma((7 * pieces,)),
            dma((lines * pieces,)), dma((lines * pieces,)), dma((7 * pieces,)), dma((7 * pieces,)),
        ],
        compiler_params=pltpu.CompilerParams(
            collective_id=0, has_side_effects=True, vmem_limit_bytes=VMEM_BYTES),
        cost_estimate=pl.CostEstimate(
            flops=2 * rows * depth * eofs, bytes_accessed=2 * depth * (rows + eofs), transcendentals=0),
    )(fields, basis)


def split(value, pieces):
    out = []
    for _ in range(pieces):
        part = value.astype(jnp.bfloat16)
        out.append(part)
        value = value - part.astype(jnp.float32)
    return out


def regime_kernel(seeds, amplitudes, fields, member_out, centers_out, composites, fbuf, member_buf, centers_buf,
                  composite_buf, load_sems, store_sems):
    days, eofs = amplitudes.shape
    regimes, points = composites.shape
    piece = days // CHUNKS
    loads = []
    for i in range(CHUNKS):
        load = pltpu.make_async_copy(fields.at[pl.ds(i * piece, piece)], fbuf.at[pl.ds(i * piece, piece)],
                                     load_sems.at[i])
        load.start()
        loads.append(load)

    turned = amplitudes[...].T
    with_ones = jnp.concatenate([turned, jnp.ones((16, days), jnp.float32)], axis=0)
    first, second, third = split(with_ones, 3)
    exact = jnp.concatenate([first, second, third], axis=1)
    pair = jnp.concatenate([first, second, first], axis=1)
    stores = []

    def store(src, dst):
        copy = pltpu.make_async_copy(src, dst, store_sems.at[len(stores)])
        copy.start()
        stores.append(copy)

    def member(columns):
        squares = []
        for c in range(regimes):
            offset = turned - columns[:, c:c + 1]
            squares.append(jnp.sum(offset * offset, axis=0, keepdims=True))
        mean_square = jnp.concatenate(squares, axis=0) * (1.0 / eofs) + 1e-05
        weights = 1.0 / mean_square
        return weights / jnp.sum(weights, axis=0, keepdims=True)

    positions = lax.broadcasted_iota(jnp.int32, (regimes, days), 1)
    rows = lax.broadcasted_iota(jnp.int32, (regimes, days), 0)
    chosen = jnp.zeros((regimes, days), jnp.int32)
    for c in range(regimes):
        chosen = jnp.where(rows == c, seeds[c], chosen)
    selector = (chosen == positions).astype(jnp.bfloat16)
    columns = lax.dot_general(exact, jnp.concatenate([selector] * 3, axis=1), NT,
                              preferred_element_type=jnp.float32)[:eofs]
    for sweep in range(ITERS):
        q = member(columns)
        high, low = split(q * q, 2)
        weights = jnp.concatenate([high, high, low], axis=1)
        sums = lax.dot_general(pair, weights, NT, preferred_element_type=jnp.float32)
        columns = sums[:eofs] / sums[eofs:eofs + 1]
        if sweep == ITERS - 1:
            flat = lax.dot_general(weights, pair, NT, preferred_element_type=jnp.float32)
            centers_buf[...] = flat[:, :eofs] / flat[:, eofs:eofs + 1]
            store(centers_buf, centers_out)
    final = member(columns)
    squares = final * final
    scale = 1.0 / jnp.sum(squares, axis=1, keepdims=True)
    weights_bf = squares.astype(jnp.bfloat16)
    member_buf[...] = final
    store(member_buf, member_out)
    for load in loads:
        load.wait()
    width = COLUMNS if points % COLUMNS == 0 else points
    for first in range(0, points, width):
        part = slice(first, first + width)
        composite_buf[:, part] = jnp.dot(
            weights_bf, fbuf[:, part], preferred_element_type=jnp.float32) * scale
        store(composite_buf.at[:, pl.ds(first, width)], composites.at[:, pl.ds(first, width)])
    for copy in stores:
        copy.wait()


def regimes_of(seed_days, amplitudes, fields):
    days, points = fields.shape
    eofs = amplitudes.shape[1]
    regimes = seed_days.shape[0]
    vmem = pl.BlockSpec(memory_space=pltpu.VMEM)
    hbm = pl.BlockSpec(memory_space=pltpu.HBM)
    member, centers, composites = pl.pallas_call(
        regime_kernel,
        out_shape=(
            jax.ShapeDtypeStruct((regimes, days), jnp.float32),
            jax.ShapeDtypeStruct((regimes, eofs), jnp.float32),
            jax.ShapeDtypeStruct((regimes, points), jnp.float32),
        ),
        in_specs=[pl.BlockSpec(memory_space=pltpu.SMEM), vmem, hbm],
        out_specs=(hbm, hbm, hbm),
        scratch_shapes=[
            pltpu.VMEM((days, points), jnp.bfloat16),
            pltpu.VMEM((regimes, days), jnp.float32),
            pltpu.VMEM((regimes, eofs), jnp.float32),
            pltpu.VMEM((regimes, points), jnp.float32),
            pltpu.SemaphoreType.DMA((CHUNKS,)),
            pltpu.SemaphoreType.DMA((2 + max(1, points // COLUMNS),)),
        ],
        compiler_params=pltpu.CompilerParams(vmem_limit_bytes=VMEM_BYTES),
        cost_estimate=pl.CostEstimate(
            flops=2 * regimes * days * points, bytes_accessed=2 * days * points, transcendentals=0),
    )(seed_days, amplitudes, fields)
    return member.T, centers, composites


def on_device(mesh, fields, eof_basis, seed_days):
    n = mesh.shape["grid"]
    day_rows = fields.shape[0]
    if n % 8 == 0 and n > 8 and day_rows % 128 == 0:
        amplitudes = summed_amplitudes(n // 8, fields, eof_basis)
    else:
        partial_value = jnp.dot(fields, eof_basis, preferred_element_type=jnp.float32)
        amplitudes = lax.psum(partial_value, "grid")
    if mesh.shape["day"] == 1 and day_rows % 128 == 0 and eof_basis.shape[1] % 128 == 0:
        return regimes_of(seed_days, amplitudes, fields)
    first = lax.axis_index("day") * day_rows
    centers = lax.psum(seed_terms(seed_days, first, amplitudes), "day")
    for sweep in range(ITERS):
        numerator, denominator = lax.psum(regime_terms(amplitudes, centers), "day")
        centers = numerator / denominator[:, None]
    member_all = member_of(amplitudes, centers)
    squares = member_all * member_all
    weights_bf = squares.astype(jnp.bfloat16)
    weighted = jnp.dot(weights_bf.T, fields, preferred_element_type=jnp.float32)
    totals, weight_sums = lax.psum((weighted, jnp.sum(squares, axis=0)), "day")
    return (member_all, centers, totals / weight_sums[:, None])


def solution(mesh):
    placed = (P("day", "grid"), P("grid", None), P())
    return jax.shard_map(
        functools.partial(on_device, mesh),
        mesh=mesh,
        in_specs=placed,
        out_specs=(P("day", None), P(), P(None, "grid")),
        check_vma=False,
    )
```

```python
import functools

import jax
import jax.numpy as jnp
from jax import lax
from jax.experimental import pallas as pl
from jax.experimental.pallas import tpu as pltpu
from jax.sharding import PartitionSpec as P

ITERS = 3
CHUNKS = 2
VMEM_BYTES = 53 * 1024 * 1024
COLUMNS = 1024
DEPTH_CHUNKS = 8
NT = (((1,), (1,)), ((), ()))


def member_of(amplitudes, centers):
    offsets = amplitudes[:, None, :] - centers[None, :, :]
    mean_square = jnp.mean(offsets * offsets, axis=2) + 1e-05
    weights = 1.0 / mean_square
    return weights / jnp.sum(weights, axis=1, keepdims=True)


def seed_terms(seed_days, first, amplitudes):
    positions = first + jnp.arange(amplitudes.shape[0], dtype=jnp.int32)
    selector = (seed_days[:, None] == positions[None, :]).astype(jnp.float32)
    return jnp.dot(selector, amplitudes, precision=lax.Precision.HIGHEST)


def regime_terms(amplitudes, centers):
    member = member_of(amplitudes, centers)
    squared = member * member
    numerator = jnp.dot(squared.T, amplitudes, precision=lax.Precision.HIGHEST)
    return (numerator, jnp.sum(squared, axis=0))


def piece_sizes(block):
    return [block - 16, 16] if block > 16 else [block]


def amplitude_kernel(lines, fields, basis, out, fbuf, bbuf, mine, parts, stack, load_sems,
                     plane_send, plane_recv, line_send, line_recv, back_send, back_recv):
    rows = out.shape[0]
    block = rows // 8
    me = lax.axis_index("grid")
    core = lax.rem(me, 2)
    px = lax.rem(me // 2, 2)
    py = lax.rem(me // 4, 2)
    line = me // 8
    flips = [(1, 1, 0), (1, 1, 1), (1, 0, 0), (1, 0, 1), (0, 1, 0), (0, 1, 1), (0, 0, 1), (0, 0, 0)]
    order = []
    for fy, fx, fc in flips:
        y = 1 - py if fy else py
        x = 1 - px if fx else px
        c = 1 - core if fc else core
        order.append((y * 2 + x) * 2 + c)
    own = order[7]

    def send(src, dst, send_sem, recv_sem, device):
        return pltpu.make_async_remote_copy(
            src_ref=src, dst_ref=dst, send_sem=send_sem, recv_sem=recv_sem,
            device_id={"grid": device}, device_id_type=pl.DeviceIdType.MESH)

    plane_peers = [line * 8 + position for position in order[:7]]
    line_steps = sorted(range(1, lines), key=lambda step: -min(step, lines - step))
    line_devices = [lax.rem(line + step, lines) * 8 + own for step in line_steps]
    line_sources = [lax.rem(line + lines - step, lines) for step in line_steps]

    barrier = pltpu.get_barrier_semaphore()
    for device in line_devices + plane_peers:
        pl.semaphore_signal(barrier, inc=1, device_id={"grid": device}, device_id_type=pl.DeviceIdType.MESH)

    depth = basis.shape[0] // DEPTH_CHUNKS
    loads = []
    for i in range(DEPTH_CHUNKS):
        part = pl.ds(i * depth, depth)
        pair = (pltpu.make_async_copy(basis.at[part], bbuf.at[part], load_sems.at[2 * i]),
                pltpu.make_async_copy(fields.at[:, part], fbuf.at[:, part], load_sems.at[2 * i + 1]))
        for load in pair:
            load.start()
        loads.append(pair)

    sizes = piece_sizes(block)
    starts = [sum(sizes[:p]) for p in range(len(sizes))]
    pieces = range(len(sizes))
    started = []

    def begin(*what):
        copy = send(*what)
        copy.start()
        started.append(copy)
        return copy

    def rows_of(p):
        return pl.ds(starts[p], sizes[p])

    total = None
    for i in range(DEPTH_CHUNKS):
        for load in loads[i]:
            load.wait()
        part = slice(i * depth, (i + 1) * depth)
        term = jnp.dot(fbuf[:, part], bbuf[part, :], preferred_element_type=jnp.float32)
        total = term if total is None else total + term
    mine[...] = total

    def block_rows(k, p):
        return pl.ds(pl.multiple_of(order[k] * block + starts[p], 8), sizes[p])

    pl.semaphore_wait(barrier, 7 + lines - 1)
    plane_copies = {}
    for p in pieces:
        for k in range(7):
            plane_copies[p, k] = begin(
                mine.at[block_rows(k, p)], parts.at[k, rows_of(p)],
                plane_send.at[p * 7 + k], plane_recv.at[p * 7 + k], plane_peers[k])

    for p in pieces:
        total = mine[block_rows(7, p), :]
        for k in reversed(range(7)):
            plane_copies[p, k].wait_recv()
            total = total + parts[k, rows_of(p), :]
        stack[line, rows_of(p), :] = total
        slot = stack.at[line, rows_of(p)]
        for step, device in enumerate(line_devices):
            begin(slot, slot, line_send.at[p * lines + step], line_recv.at[p * lines + line], device)

    def drain():
        while started:
            started.pop().wait_send()

    def place(k, p):
        return out.at[block_rows(k, p)]

    line_copies = started[-len(pieces) * (lines - 1):]
    del started[-len(pieces) * (lines - 1):]
    drain()
    for p in pieces:
        for step, source in enumerate(line_sources):
            slot = stack.at[source, rows_of(p)]
            send(slot, slot, line_send.at[p * lines + step], line_recv.at[p * lines + source],
                 source * 8 + own).wait_recv()
        total = stack[0, rows_of(p), :]
        for j in range(1, lines):
            total = total + stack[j, rows_of(p), :]
        place(7, p)[...] = total
        for k in range(7):
            begin(place(7, p), place(7, p), back_send.at[p * 7 + k], back_recv.at[p * 7 + k], plane_peers[k])
    for copy in line_copies:
        copy.wait_send()
    for p in pieces:
        for k in reversed(range(7)):
            send(place(k, p), place(k, p), back_send.at[p * 7 + k], back_recv.at[p * 7 + k],
                 plane_peers[k]).wait_recv()
    drain()


def summed_amplitudes(lines, fields, basis):
    rows, depth = fields.shape
    eofs = basis.shape[1]
    block = rows // 8
    pieces = len(piece_sizes(block))
    dma = pltpu.SemaphoreType.DMA
    return pl.pallas_call(
        functools.partial(amplitude_kernel, lines),
        out_shape=jax.ShapeDtypeStruct((rows, eofs), jnp.float32),
        in_specs=[pl.BlockSpec(memory_space=pltpu.HBM)] * 2,
        out_specs=pl.BlockSpec(memory_space=pltpu.VMEM),
        scratch_shapes=[
            pltpu.VMEM((rows, depth), jnp.bfloat16),
            pltpu.VMEM((depth, eofs), jnp.bfloat16),
            pltpu.VMEM((rows, eofs), jnp.float32),
            pltpu.VMEM((7, block, eofs), jnp.float32),
            pltpu.VMEM((lines, block, eofs), jnp.float32),
            dma((2 * DEPTH_CHUNKS,)), dma((7 * pieces,)), dma((7 * pieces,)),
            dma((lines * pieces,)), dma((lines * pieces,)), dma((7 * pieces,)), dma((7 * pieces,)),
        ],
        compiler_params=pltpu.CompilerParams(
            collective_id=0, has_side_effects=True, vmem_limit_bytes=VMEM_BYTES),
        cost_estimate=pl.CostEstimate(
            flops=2 * rows * depth * eofs, bytes_accessed=2 * depth * (rows + eofs), transcendentals=0),
    )(fields, basis)


def split(value, pieces):
    out = []
    for _ in range(pieces):
        part = value.astype(jnp.bfloat16)
        out.append(part)
        value = value - part.astype(jnp.float32)
    return out


def regime_kernel(seeds, amplitudes, fields, member_out, centers_out, composites, fbuf, member_buf, centers_buf,
                  composite_buf, load_sems, store_sems):
    days, eofs = amplitudes.shape
    regimes, points = composites.shape
    piece = days // CHUNKS
    loads = []
    for i in range(CHUNKS):
        load = pltpu.make_async_copy(fields.at[pl.ds(i * piece, piece)], fbuf.at[pl.ds(i * piece, piece)],
                                     load_sems.at[i])
        load.start()
        loads.append(load)

    turned = amplitudes[...].T
    with_ones = jnp.concatenate([turned, jnp.ones((16, days), jnp.float32)], axis=0)
    first, second, third = split(with_ones, 3)
    exact = jnp.concatenate([first, second, third], axis=1)
    pair = jnp.concatenate([first, second, first], axis=1)
    stores = []

    def store(src, dst):
        copy = pltpu.make_async_copy(src, dst, store_sems.at[len(stores)])
        copy.start()
        stores.append(copy)

    def member(columns):
        squares = []
        for c in range(regimes):
            offset = turned - columns[:, c:c + 1]
            squares.append(jnp.sum(offset * offset, axis=0, keepdims=True))
        mean_square = jnp.concatenate(squares, axis=0) * (1.0 / eofs) + 1e-05
        weights = 1.0 / mean_square
        return weights / jnp.sum(weights, axis=0, keepdims=True)

    positions = lax.broadcasted_iota(jnp.int32, (regimes, days), 1)
    rows = lax.broadcasted_iota(jnp.int32, (regimes, days), 0)
    chosen = jnp.zeros((regimes, days), jnp.int32)
    for c in range(regimes):
        chosen = jnp.where(rows == c, seeds[c], chosen)
    selector = (chosen == positions).astype(jnp.bfloat16)
    columns = lax.dot_general(exact, jnp.concatenate([selector] * 3, axis=1), NT,
                              preferred_element_type=jnp.float32)[:eofs]
    for sweep in range(ITERS):
        q = member(columns)
        high, low = split(q * q, 2)
        weights = jnp.concatenate([high, high, low], axis=1)
        sums = lax.dot_general(pair, weights, NT, preferred_element_type=jnp.float32)
        columns = sums[:eofs] / sums[eofs:eofs + 1]
        if sweep == ITERS - 1:
            flat = lax.dot_general(weights, pair, NT, preferred_element_type=jnp.float32)
            centers_buf[...] = flat[:, :eofs] / flat[:, eofs:eofs + 1]
            store(centers_buf, centers_out)
    final = member(columns)
    squares = final * final
    scale = 1.0 / jnp.sum(squares, axis=1, keepdims=True)
    weights_bf = squares.astype(jnp.bfloat16)
    member_buf[...] = final
    store(member_buf, member_out)
    for load in loads:
        load.wait()
    width = COLUMNS if points % COLUMNS == 0 else points
    for first in range(0, points, width):
        part = slice(first, first + width)
        composite_buf[:, part] = jnp.dot(
            weights_bf, fbuf[:, part], preferred_element_type=jnp.float32) * scale
        store(composite_buf.at[:, pl.ds(first, width)], composites.at[:, pl.ds(first, width)])
    for copy in stores:
        copy.wait()


def regimes_of(seed_days, amplitudes, fields):
    days, points = fields.shape
    eofs = amplitudes.shape[1]
    regimes = seed_days.shape[0]
    vmem = pl.BlockSpec(memory_space=pltpu.VMEM)
    hbm = pl.BlockSpec(memory_space=pltpu.HBM)
    member, centers, composites = pl.pallas_call(
        regime_kernel,
        out_shape=(
            jax.ShapeDtypeStruct((regimes, days), jnp.float32),
            jax.ShapeDtypeStruct((regimes, eofs), jnp.float32),
            jax.ShapeDtypeStruct((regimes, points), jnp.float32),
        ),
        in_specs=[pl.BlockSpec(memory_space=pltpu.SMEM), vmem, hbm],
        out_specs=(hbm, hbm, hbm),
        scratch_shapes=[
            pltpu.VMEM((days, points), jnp.bfloat16),
            pltpu.VMEM((regimes, days), jnp.float32),
            pltpu.VMEM((regimes, eofs), jnp.float32),
            pltpu.VMEM((regimes, points), jnp.float32),
            pltpu.SemaphoreType.DMA((CHUNKS,)),
            pltpu.SemaphoreType.DMA((2 + max(1, points // COLUMNS),)),
        ],
        compiler_params=pltpu.CompilerParams(vmem_limit_bytes=VMEM_BYTES),
        cost_estimate=pl.CostEstimate(
            flops=2 * regimes * days * points, bytes_accessed=2 * days * points, transcendentals=0),
    )(seed_days, amplitudes, fields)
    return member.T, centers, composites


def on_device(mesh, fields, eof_basis, seed_days):
    n = mesh.shape["grid"]
    day_rows = fields.shape[0]
    if n % 8 == 0 and n > 8 and day_rows % 128 == 0 and fields.shape[1] % (256 * DEPTH_CHUNKS) == 0:
        amplitudes = summed_amplitudes(n // 8, fields, eof_basis)
    else:
        partial_value = jnp.dot(fields, eof_basis, preferred_element_type=jnp.float32)
        amplitudes = lax.psum(partial_value, "grid")
    if mesh.shape["day"] == 1 and day_rows % 128 == 0 and eof_basis.shape[1] % 128 == 0:
        return regimes_of(seed_days, amplitudes, fields)
    first = lax.axis_index("day") * day_rows
    centers = lax.psum(seed_terms(seed_days, first, amplitudes), "day")
    for sweep in range(ITERS):
        numerator, denominator = lax.psum(regime_terms(amplitudes, centers), "day")
        centers = numerator / denominator[:, None]
    member_all = member_of(amplitudes, centers)
    squares = member_all * member_all
    weights_bf = squares.astype(jnp.bfloat16)
    weighted = jnp.dot(weights_bf.T, fields, preferred_element_type=jnp.float32)
    totals, weight_sums = lax.psum((weighted, jnp.sum(squares, axis=0)), "day")
    return (member_all, centers, totals / weight_sums[:, None])


def solution(mesh):
    placed = (P("day", "grid"), P("grid", None), P())
    return jax.shard_map(
        functools.partial(on_device, mesh),
        mesh=mesh,
        in_specs=placed,
        out_specs=(P("day", None), P(), P(None, "grid")),
        check_vma=False,
    )
```

```python
import functools

import jax
import jax.numpy as jnp
from jax import lax
from jax.experimental import pallas as pl
from jax.experimental.pallas import tpu as pltpu
from jax.sharding import PartitionSpec as P

ITERS = 3
CHUNKS = 2
VMEM_BYTES = 53 * 1024 * 1024
COLUMNS = 1024
NT = (((1,), (1,)), ((), ()))


def member_of(amplitudes, centers):
    offsets = amplitudes[:, None, :] - centers[None, :, :]
    mean_square = jnp.mean(offsets * offsets, axis=2) + 1e-05
    weights = 1.0 / mean_square
    return weights / jnp.sum(weights, axis=1, keepdims=True)


def seed_terms(seed_days, first, amplitudes):
    positions = first + jnp.arange(amplitudes.shape[0], dtype=jnp.int32)
    selector = (seed_days[:, None] == positions[None, :]).astype(jnp.float32)
    return jnp.dot(selector, amplitudes, precision=lax.Precision.HIGHEST)


def regime_terms(amplitudes, centers):
    member = member_of(amplitudes, centers)
    squared = member * member
    numerator = jnp.dot(squared.T, amplitudes, precision=lax.Precision.HIGHEST)
    return (numerator, jnp.sum(squared, axis=0))


def piece_sizes(block):
    return [16] * (block // 16)


def amplitude_kernel(lines, fields, basis, out, fbuf, bbuf, mine, parts, stack, load_sems,
                     plane_send, plane_recv, line_send, line_recv, back_send, back_recv):
    rows = out.shape[0]
    block = rows // 8
    me = lax.axis_index("grid")
    core = lax.rem(me, 2)
    px = lax.rem(me // 2, 2)
    py = lax.rem(me // 4, 2)
    line = me // 8
    flips = [(1, 1, 0), (1, 1, 1), (1, 0, 0), (1, 0, 1), (0, 1, 0), (0, 1, 1), (0, 0, 1), (0, 0, 0)]
    order = []
    for fy, fx, fc in flips:
        y = 1 - py if fy else py
        x = 1 - px if fx else px
        c = 1 - core if fc else core
        order.append((y * 2 + x) * 2 + c)
    own = order[7]

    def send(src, dst, send_sem, recv_sem, device):
        return pltpu.make_async_remote_copy(
            src_ref=src, dst_ref=dst, send_sem=send_sem, recv_sem=recv_sem,
            device_id={"grid": device}, device_id_type=pl.DeviceIdType.MESH)

    plane_peers = [line * 8 + position for position in order[:7]]
    line_steps = sorted(range(1, lines), key=lambda step: -min(step, lines - step))
    line_devices = [lax.rem(line + step, lines) * 8 + own for step in line_steps]
    line_sources = [lax.rem(line + lines - step, lines) for step in line_steps]

    barrier = pltpu.get_barrier_semaphore()
    for device in line_devices + plane_peers:
        pl.semaphore_signal(barrier, inc=1, device_id={"grid": device}, device_id_type=pl.DeviceIdType.MESH)

    sizes = piece_sizes(block)
    starts = [sum(sizes[:p]) for p in range(len(sizes))]
    pieces = range(len(sizes))
    basis_load = pltpu.make_async_copy(basis, bbuf, load_sems.at[0])
    basis_load.start()
    loads = {}
    for p in pieces:
        for k in range(8):
            first = pl.multiple_of(order[k] * block + starts[p], 16)
            load = pltpu.make_async_copy(
                fields.at[pl.ds(first, sizes[p])], fbuf.at[pl.ds(8 * starts[p] + k * sizes[p], sizes[p])],
                load_sems.at[1 + p * 8 + k])
            load.start()
            loads[p, k] = load

    started = []

    def begin(*what):
        copy = send(*what)
        copy.start()
        started.append(copy)
        return copy

    def rows_of(p):
        return pl.ds(starts[p], sizes[p])

    basis_load.wait()
    plane_copies = {}
    for p in pieces:
        for k in range(8):
            loads[p, k].wait()
        span = slice(8 * starts[p], 8 * (starts[p] + sizes[p]))
        mine[span, :] = jnp.dot(fbuf[span, :], bbuf[...], preferred_element_type=jnp.float32)
        if p == 0:
            pl.semaphore_wait(barrier, 7 + lines - 1)
        for k in range(7):
            plane_copies[p, k] = begin(
                mine.at[pl.ds(8 * starts[p] + k * sizes[p], sizes[p])], parts.at[k, rows_of(p)],
                plane_send.at[p * 7 + k], plane_recv.at[p * 7 + k], plane_peers[k])

    for p in pieces:
        first = 8 * starts[p] + 7 * sizes[p]
        total = mine[first:first + sizes[p], :]
        for k in reversed(range(7)):
            plane_copies[p, k].wait_recv()
            total = total + parts[k, rows_of(p), :]
        stack[line, rows_of(p), :] = total
        slot = stack.at[line, rows_of(p)]
        for step, device in enumerate(line_devices):
            begin(slot, slot, line_send.at[p * lines + step], line_recv.at[p * lines + line], device)

    def drain():
        while started:
            started.pop().wait_send()

    def place(k, p):
        return out.at[pl.ds(pl.multiple_of(order[k] * block + starts[p], 8), sizes[p])]

    line_copies = started[-len(pieces) * (lines - 1):]
    del started[-len(pieces) * (lines - 1):]
    drain()
    for p in pieces:
        for step, source in enumerate(line_sources):
            slot = stack.at[source, rows_of(p)]
            send(slot, slot, line_send.at[p * lines + step], line_recv.at[p * lines + source],
                 source * 8 + own).wait_recv()
        total = stack[0, rows_of(p), :]
        for j in range(1, lines):
            total = total + stack[j, rows_of(p), :]
        place(7, p)[...] = total
        for k in range(7):
            begin(place(7, p), place(7, p), back_send.at[p * 7 + k], back_recv.at[p * 7 + k], plane_peers[k])
    for copy in line_copies:
        copy.wait_send()
    for p in pieces:
        for k in reversed(range(7)):
            send(place(k, p), place(k, p), back_send.at[p * 7 + k], back_recv.at[p * 7 + k],
                 plane_peers[k]).wait_recv()
    drain()


def summed_amplitudes(lines, fields, basis):
    rows, depth = fields.shape
    eofs = basis.shape[1]
    block = rows // 8
    pieces = len(piece_sizes(block))
    dma = pltpu.SemaphoreType.DMA
    return pl.pallas_call(
        functools.partial(amplitude_kernel, lines),
        out_shape=jax.ShapeDtypeStruct((rows, eofs), jnp.float32),
        in_specs=[pl.BlockSpec(memory_space=pltpu.HBM)] * 2,
        out_specs=pl.BlockSpec(memory_space=pltpu.VMEM),
        scratch_shapes=[
            pltpu.VMEM((rows, depth), jnp.bfloat16),
            pltpu.VMEM((depth, eofs), jnp.bfloat16),
            pltpu.VMEM((rows, eofs), jnp.float32),
            pltpu.VMEM((7, block, eofs), jnp.float32),
            pltpu.VMEM((lines, block, eofs), jnp.float32),
            dma((1 + 8 * pieces,)), dma((7 * pieces,)), dma((7 * pieces,)),
            dma((lines * pieces,)), dma((lines * pieces,)), dma((7 * pieces,)), dma((7 * pieces,)),
        ],
        compiler_params=pltpu.CompilerParams(
            collective_id=0, has_side_effects=True, vmem_limit_bytes=VMEM_BYTES),
        cost_estimate=pl.CostEstimate(
            flops=2 * rows * depth * eofs, bytes_accessed=2 * depth * (rows + eofs), transcendentals=0),
    )(fields, basis)


def split(value, pieces):
    out = []
    for _ in range(pieces):
        part = value.astype(jnp.bfloat16)
        out.append(part)
        value = value - part.astype(jnp.float32)
    return out


def regime_kernel(seeds, amplitudes, fields, member_out, centers_out, composites, fbuf, member_buf, centers_buf,
                  composite_buf, load_sems, store_sems):
    days, eofs = amplitudes.shape
    regimes, points = composites.shape
    piece = days // CHUNKS
    loads = []
    for i in range(CHUNKS):
        load = pltpu.make_async_copy(fields.at[pl.ds(i * piece, piece)], fbuf.at[pl.ds(i * piece, piece)],
                                     load_sems.at[i])
        load.start()
        loads.append(load)

    turned = amplitudes[...].T
    with_ones = jnp.concatenate([turned, jnp.ones((16, days), jnp.float32)], axis=0)
    first, second, third = split(with_ones, 3)
    exact = jnp.concatenate([first, second, third], axis=1)
    pair = jnp.concatenate([first, second, first], axis=1)
    stores = []

    def store(src, dst):
        copy = pltpu.make_async_copy(src, dst, store_sems.at[len(stores)])
        copy.start()
        stores.append(copy)

    def member(columns):
        squares = []
        for c in range(regimes):
            offset = turned - columns[:, c:c + 1]
            squares.append(jnp.sum(offset * offset, axis=0, keepdims=True))
        mean_square = jnp.concatenate(squares, axis=0) * (1.0 / eofs) + 1e-05
        weights = 1.0 / mean_square
        return weights / jnp.sum(weights, axis=0, keepdims=True)

    positions = lax.broadcasted_iota(jnp.int32, (regimes, days), 1)
    rows = lax.broadcasted_iota(jnp.int32, (regimes, days), 0)
    chosen = jnp.zeros((regimes, days), jnp.int32)
    for c in range(regimes):
        chosen = jnp.where(rows == c, seeds[c], chosen)
    selector = (chosen == positions).astype(jnp.bfloat16)
    columns = lax.dot_general(exact, jnp.concatenate([selector] * 3, axis=1), NT,
                              preferred_element_type=jnp.float32)[:eofs]
    for sweep in range(ITERS):
        q = member(columns)
        high, low = split(q * q, 2)
        weights = jnp.concatenate([high, high, low], axis=1)
        sums = lax.dot_general(pair, weights, NT, preferred_element_type=jnp.float32)
        columns = sums[:eofs] / sums[eofs:eofs + 1]
        if sweep == ITERS - 1:
            flat = lax.dot_general(weights, pair, NT, preferred_element_type=jnp.float32)
            centers_buf[...] = flat[:, :eofs] / flat[:, eofs:eofs + 1]
            store(centers_buf, centers_out)
    final = member(columns)
    squares = final * final
    scale = 1.0 / jnp.sum(squares, axis=1, keepdims=True)
    weights_bf = squares.astype(jnp.bfloat16)
    member_buf[...] = final
    store(member_buf, member_out)
    for load in loads:
        load.wait()
    width = COLUMNS if points % COLUMNS == 0 else points
    for first in range(0, points, width):
        part = slice(first, first + width)
        composite_buf[:, part] = jnp.dot(
            weights_bf, fbuf[:, part], preferred_element_type=jnp.float32) * scale
        store(composite_buf.at[:, pl.ds(first, width)], composites.at[:, pl.ds(first, width)])
    for copy in stores:
        copy.wait()


def regimes_of(seed_days, amplitudes, fields):
    days, points = fields.shape
    eofs = amplitudes.shape[1]
    regimes = seed_days.shape[0]
    vmem = pl.BlockSpec(memory_space=pltpu.VMEM)
    hbm = pl.BlockSpec(memory_space=pltpu.HBM)
    member, centers, composites = pl.pallas_call(
        regime_kernel,
        out_shape=(
            jax.ShapeDtypeStruct((regimes, days), jnp.float32),
            jax.ShapeDtypeStruct((regimes, eofs), jnp.float32),
            jax.ShapeDtypeStruct((regimes, points), jnp.float32),
        ),
        in_specs=[pl.BlockSpec(memory_space=pltpu.SMEM), vmem, hbm],
        out_specs=(hbm, hbm, hbm),
        scratch_shapes=[
            pltpu.VMEM((days, points), jnp.bfloat16),
            pltpu.VMEM((regimes, days), jnp.float32),
            pltpu.VMEM((regimes, eofs), jnp.float32),
            pltpu.VMEM((regimes, points), jnp.float32),
            pltpu.SemaphoreType.DMA((CHUNKS,)),
            pltpu.SemaphoreType.DMA((2 + max(1, points // COLUMNS),)),
        ],
        compiler_params=pltpu.CompilerParams(vmem_limit_bytes=VMEM_BYTES),
        cost_estimate=pl.CostEstimate(
            flops=2 * regimes * days * points, bytes_accessed=2 * days * points, transcendentals=0),
    )(seed_days, amplitudes, fields)
    return member.T, centers, composites


def on_device(mesh, fields, eof_basis, seed_days):
    n = mesh.shape["grid"]
    day_rows = fields.shape[0]
    if n % 8 == 0 and n > 8 and day_rows % 128 == 0:
        amplitudes = summed_amplitudes(n // 8, fields, eof_basis)
    else:
        partial_value = jnp.dot(fields, eof_basis, preferred_element_type=jnp.float32)
        amplitudes = lax.psum(partial_value, "grid")
    if mesh.shape["day"] == 1 and day_rows % 128 == 0 and eof_basis.shape[1] % 128 == 0:
        return regimes_of(seed_days, amplitudes, fields)
    first = lax.axis_index("day") * day_rows
    centers = lax.psum(seed_terms(seed_days, first, amplitudes), "day")
    for sweep in range(ITERS):
        numerator, denominator = lax.psum(regime_terms(amplitudes, centers), "day")
        centers = numerator / denominator[:, None]
    member_all = member_of(amplitudes, centers)
    squares = member_all * member_all
    weights_bf = squares.astype(jnp.bfloat16)
    weighted = jnp.dot(weights_bf.T, fields, preferred_element_type=jnp.float32)
    totals, weight_sums = lax.psum((weighted, jnp.sum(squares, axis=0)), "day")
    return (member_all, centers, totals / weight_sums[:, None])


def solution(mesh):
    placed = (P("day", "grid"), P("grid", None), P())
    return jax.shard_map(
        functools.partial(on_device, mesh),
        mesh=mesh,
        in_specs=placed,
        out_specs=(P("day", None), P(), P(None, "grid")),
        check_vma=False,
    )
```

```python
import functools

import jax
import jax.numpy as jnp
from jax import lax
from jax.experimental import pallas as pl
from jax.experimental.pallas import tpu as pltpu
from jax.sharding import PartitionSpec as P

ITERS = 3
CHUNKS = 2
VMEM_BYTES = 53 * 1024 * 1024
COLUMNS = 1024
BASIS_COPIES = 4
NT = (((1,), (1,)), ((), ()))


def member_of(amplitudes, centers):
    offsets = amplitudes[:, None, :] - centers[None, :, :]
    mean_square = jnp.mean(offsets * offsets, axis=2) + 1e-05
    weights = 1.0 / mean_square
    return weights / jnp.sum(weights, axis=1, keepdims=True)


def seed_terms(seed_days, first, amplitudes):
    positions = first + jnp.arange(amplitudes.shape[0], dtype=jnp.int32)
    selector = (seed_days[:, None] == positions[None, :]).astype(jnp.float32)
    return jnp.dot(selector, amplitudes, precision=lax.Precision.HIGHEST)


def regime_terms(amplitudes, centers):
    member = member_of(amplitudes, centers)
    squared = member * member
    numerator = jnp.dot(squared.T, amplitudes, precision=lax.Precision.HIGHEST)
    return (numerator, jnp.sum(squared, axis=0))


def piece_sizes(block):
    return [16] * (block // 16)


def amplitude_kernel(lines, fields, basis, out, fbuf, bbuf, mine, parts, stack, load_sems,
                     plane_send, plane_recv, line_send, line_recv, back_send, back_recv):
    rows = out.shape[0]
    block = rows // 8
    me = lax.axis_index("grid")
    core = lax.rem(me, 2)
    px = lax.rem(me // 2, 2)
    py = lax.rem(me // 4, 2)
    line = me // 8
    flips = [(1, 1, 0), (1, 1, 1), (1, 0, 0), (1, 0, 1), (0, 1, 0), (0, 1, 1), (0, 0, 1), (0, 0, 0)]
    order = []
    for fy, fx, fc in flips:
        y = 1 - py if fy else py
        x = 1 - px if fx else px
        c = 1 - core if fc else core
        order.append((y * 2 + x) * 2 + c)
    own = order[7]

    def send(src, dst, send_sem, recv_sem, device):
        return pltpu.make_async_remote_copy(
            src_ref=src, dst_ref=dst, send_sem=send_sem, recv_sem=recv_sem,
            device_id={"grid": device}, device_id_type=pl.DeviceIdType.MESH)

    plane_peers = [line * 8 + position for position in order[:7]]
    line_steps = sorted(range(1, lines), key=lambda step: -min(step, lines - step))
    line_devices = [lax.rem(line + step, lines) * 8 + own for step in line_steps]
    line_sources = [lax.rem(line + lines - step, lines) for step in line_steps]

    barrier = pltpu.get_barrier_semaphore()
    for device in line_devices + plane_peers:
        pl.semaphore_signal(barrier, inc=1, device_id={"grid": device}, device_id_type=pl.DeviceIdType.MESH)

    sizes = piece_sizes(block)
    starts = [sum(sizes[:p]) for p in range(len(sizes))]
    pieces = range(len(sizes))
    depth = basis.shape[0] // BASIS_COPIES
    basis_loads = []
    for i in range(BASIS_COPIES):
        part = pl.ds(i * depth, depth)
        load = pltpu.make_async_copy(basis.at[part], bbuf.at[part], load_sems.at[i])
        load.start()
        basis_loads.append(load)
    loads = {}
    for p in pieces:
        for k in range(8):
            first = pl.multiple_of(order[k] * block + starts[p], 16)
            load = pltpu.make_async_copy(
                fields.at[pl.ds(first, sizes[p])], fbuf.at[pl.ds(8 * starts[p] + k * sizes[p], sizes[p])],
                load_sems.at[BASIS_COPIES + p * 8 + k])
            load.start()
            loads[p, k] = load

    started = []

    def begin(*what):
        copy = send(*what)
        copy.start()
        started.append(copy)
        return copy

    def rows_of(p):
        return pl.ds(starts[p], sizes[p])

    for load in basis_loads:
        load.wait()
    plane_copies = {}
    for p in pieces:
        for k in range(8):
            loads[p, k].wait()
        span = slice(8 * starts[p], 8 * (starts[p] + sizes[p]))
        mine[span, :] = jnp.dot(fbuf[span, :], bbuf[...], preferred_element_type=jnp.float32)
        if p == 0:
            pl.semaphore_wait(barrier, 7 + lines - 1)
        for k in range(7):
            plane_copies[p, k] = begin(
                mine.at[pl.ds(8 * starts[p] + k * sizes[p], sizes[p])], parts.at[k, rows_of(p)],
                plane_send.at[p * 7 + k], plane_recv.at[p * 7 + k], plane_peers[k])

    for p in pieces:
        first = 8 * starts[p] + 7 * sizes[p]
        total = mine[first:first + sizes[p], :]
        for k in reversed(range(7)):
            plane_copies[p, k].wait_recv()
            total = total + parts[k, rows_of(p), :]
        stack[line, rows_of(p), :] = total
        slot = stack.at[line, rows_of(p)]
        for step, device in enumerate(line_devices):
            begin(slot, slot, line_send.at[p * lines + step], line_recv.at[p * lines + line], device)

    def drain():
        while started:
            started.pop().wait_send()

    def place(k, p):
        return out.at[pl.ds(pl.multiple_of(order[k] * block + starts[p], 8), sizes[p])]

    line_copies = started[-len(pieces) * (lines - 1):]
    del started[-len(pieces) * (lines - 1):]
    drain()
    for p in pieces:
        for step, source in enumerate(line_sources):
            slot = stack.at[source, rows_of(p)]
            send(slot, slot, line_send.at[p * lines + step], line_recv.at[p * lines + source],
                 source * 8 + own).wait_recv()
        total = stack[0, rows_of(p), :]
        for j in range(1, lines):
            total = total + stack[j, rows_of(p), :]
        place(7, p)[...] = total
        for k in range(7):
            begin(place(7, p), place(7, p), back_send.at[p * 7 + k], back_recv.at[p * 7 + k], plane_peers[k])
    for copy in line_copies:
        copy.wait_send()
    for p in pieces:
        for k in reversed(range(7)):
            send(place(k, p), place(k, p), back_send.at[p * 7 + k], back_recv.at[p * 7 + k],
                 plane_peers[k]).wait_recv()
    drain()


def summed_amplitudes(lines, fields, basis):
    rows, depth = fields.shape
    eofs = basis.shape[1]
    block = rows // 8
    pieces = len(piece_sizes(block))
    dma = pltpu.SemaphoreType.DMA
    return pl.pallas_call(
        functools.partial(amplitude_kernel, lines),
        out_shape=jax.ShapeDtypeStruct((rows, eofs), jnp.float32),
        in_specs=[pl.BlockSpec(memory_space=pltpu.HBM)] * 2,
        out_specs=pl.BlockSpec(memory_space=pltpu.VMEM),
        scratch_shapes=[
            pltpu.VMEM((rows, depth), jnp.bfloat16),
            pltpu.VMEM((depth, eofs), jnp.bfloat16),
            pltpu.VMEM((rows, eofs), jnp.float32),
            pltpu.VMEM((7, block, eofs), jnp.float32),
            pltpu.VMEM((lines, block, eofs), jnp.float32),
            dma((BASIS_COPIES + 8 * pieces,)), dma((7 * pieces,)), dma((7 * pieces,)),
            dma((lines * pieces,)), dma((lines * pieces,)), dma((7 * pieces,)), dma((7 * pieces,)),
        ],
        compiler_params=pltpu.CompilerParams(
            collective_id=0, has_side_effects=True, vmem_limit_bytes=VMEM_BYTES),
        cost_estimate=pl.CostEstimate(
            flops=2 * rows * depth * eofs, bytes_accessed=2 * depth * (rows + eofs), transcendentals=0),
    )(fields, basis)


def split(value, pieces):
    out = []
    for _ in range(pieces):
        part = value.astype(jnp.bfloat16)
        out.append(part)
        value = value - part.astype(jnp.float32)
    return out


def regime_kernel(seeds, amplitudes, fields, member_out, centers_out, composites, fbuf, member_buf, centers_buf,
                  composite_buf, load_sems, store_sems):
    days, eofs = amplitudes.shape
    regimes, points = composites.shape
    piece = days // CHUNKS
    loads = []
    for i in range(CHUNKS):
        load = pltpu.make_async_copy(fields.at[pl.ds(i * piece, piece)], fbuf.at[pl.ds(i * piece, piece)],
                                     load_sems.at[i])
        load.start()
        loads.append(load)

    turned = amplitudes[...].T
    with_ones = jnp.concatenate([turned, jnp.ones((16, days), jnp.float32)], axis=0)
    first, second, third = split(with_ones, 3)
    exact = jnp.concatenate([first, second, third], axis=1)
    pair = jnp.concatenate([first, second, first], axis=1)
    stores = []

    def store(src, dst):
        copy = pltpu.make_async_copy(src, dst, store_sems.at[len(stores)])
        copy.start()
        stores.append(copy)

    def member(columns):
        squares = []
        for c in range(regimes):
            offset = turned - columns[:, c:c + 1]
            squares.append(jnp.sum(offset * offset, axis=0, keepdims=True))
        mean_square = jnp.concatenate(squares, axis=0) * (1.0 / eofs) + 1e-05
        weights = 1.0 / mean_square
        return weights / jnp.sum(weights, axis=0, keepdims=True)

    positions = lax.broadcasted_iota(jnp.int32, (regimes, days), 1)
    rows = lax.broadcasted_iota(jnp.int32, (regimes, days), 0)
    chosen = jnp.zeros((regimes, days), jnp.int32)
    for c in range(regimes):
        chosen = jnp.where(rows == c, seeds[c], chosen)
    selector = (chosen == positions).astype(jnp.bfloat16)
    columns = lax.dot_general(exact, jnp.concatenate([selector] * 3, axis=1), NT,
                              preferred_element_type=jnp.float32)[:eofs]
    for sweep in range(ITERS):
        q = member(columns)
        high, low = split(q * q, 2)
        weights = jnp.concatenate([high, high, low], axis=1)
        sums = lax.dot_general(pair, weights, NT, preferred_element_type=jnp.float32)
        columns = sums[:eofs] / sums[eofs:eofs + 1]
        if sweep == ITERS - 1:
            flat = lax.dot_general(weights, pair, NT, preferred_element_type=jnp.float32)
            centers_buf[...] = flat[:, :eofs] / flat[:, eofs:eofs + 1]
            store(centers_buf, centers_out)
    final = member(columns)
    squares = final * final
    scale = 1.0 / jnp.sum(squares, axis=1, keepdims=True)
    weights_bf = squares.astype(jnp.bfloat16)
    member_buf[...] = final
    store(member_buf, member_out)
    for load in loads:
        load.wait()
    width = COLUMNS if points % COLUMNS == 0 else points
    for first in range(0, points, width):
        part = slice(first, first + width)
        composite_buf[:, part] = jnp.dot(
            weights_bf, fbuf[:, part], preferred_element_type=jnp.float32) * scale
        store(composite_buf.at[:, pl.ds(first, width)], composites.at[:, pl.ds(first, width)])
    for copy in stores:
        copy.wait()


def regimes_of(seed_days, amplitudes, fields):
    days, points = fields.shape
    eofs = amplitudes.shape[1]
    regimes = seed_days.shape[0]
    vmem = pl.BlockSpec(memory_space=pltpu.VMEM)
    hbm = pl.BlockSpec(memory_space=pltpu.HBM)
    member, centers, composites = pl.pallas_call(
        regime_kernel,
        out_shape=(
            jax.ShapeDtypeStruct((regimes, days), jnp.float32),
            jax.ShapeDtypeStruct((regimes, eofs), jnp.float32),
            jax.ShapeDtypeStruct((regimes, points), jnp.float32),
        ),
        in_specs=[pl.BlockSpec(memory_space=pltpu.SMEM), vmem, hbm],
        out_specs=(hbm, hbm, hbm),
        scratch_shapes=[
            pltpu.VMEM((days, points), jnp.bfloat16),
            pltpu.VMEM((regimes, days), jnp.float32),
            pltpu.VMEM((regimes, eofs), jnp.float32),
            pltpu.VMEM((regimes, points), jnp.float32),
            pltpu.SemaphoreType.DMA((CHUNKS,)),
            pltpu.SemaphoreType.DMA((2 + max(1, points // COLUMNS),)),
        ],
        compiler_params=pltpu.CompilerParams(vmem_limit_bytes=VMEM_BYTES),
        cost_estimate=pl.CostEstimate(
            flops=2 * regimes * days * points, bytes_accessed=2 * days * points, transcendentals=0),
    )(seed_days, amplitudes, fields)
    return member.T, centers, composites


def on_device(mesh, fields, eof_basis, seed_days):
    n = mesh.shape["grid"]
    day_rows = fields.shape[0]
    if n % 8 == 0 and n > 8 and day_rows % 128 == 0 and eof_basis.shape[0] % (16 * BASIS_COPIES) == 0:
        amplitudes = summed_amplitudes(n // 8, fields, eof_basis)
    else:
        partial_value = jnp.dot(fields, eof_basis, preferred_element_type=jnp.float32)
        amplitudes = lax.psum(partial_value, "grid")
    if mesh.shape["day"] == 1 and day_rows % 128 == 0 and eof_basis.shape[1] % 128 == 0:
        return regimes_of(seed_days, amplitudes, fields)
    first = lax.axis_index("day") * day_rows
    centers = lax.psum(seed_terms(seed_days, first, amplitudes), "day")
    for sweep in range(ITERS):
        numerator, denominator = lax.psum(regime_terms(amplitudes, centers), "day")
        centers = numerator / denominator[:, None]
    member_all = member_of(amplitudes, centers)
    squares = member_all * member_all
    weights_bf = squares.astype(jnp.bfloat16)
    weighted = jnp.dot(weights_bf.T, fields, preferred_element_type=jnp.float32)
    totals, weight_sums = lax.psum((weighted, jnp.sum(squares, axis=0)), "day")
    return (member_all, centers, totals / weight_sums[:, None])


def solution(mesh):
    placed = (P("day", "grid"), P("grid", None), P())
    return jax.shard_map(
        functools.partial(on_device, mesh),
        mesh=mesh,
        in_specs=placed,
        out_specs=(P("day", None), P(), P(None, "grid")),
        check_vma=False,
    )
```
